256 devices in a mesh: dp: 16 (over y, x_hi, core), ctx: 16 (over z, x_lo).
Axes of the slice: x: 4 (x_hi: 2, x_lo: 2; x = x_hi * 2 + x_lo), y: 4, z: 8, core: 2. Of those that a mesh axis runs over, the one named last changes fastest.
Arguments:
- queries: bfloat16 [16, 8192, 640], P('dp', 'ctx'), may hold values from -6 to 6
- keys: bfloat16 [16, 8192, 640], P('dp', 'ctx'), may hold values from -6 to 6
- values: bfloat16 [16, 8192, 640], P('dp', 'ctx'), may hold values from -16 to 16
- grad_out: bfloat16 [16, 8192, 1280], P('dp', 'ctx'), may hold values from -6 to 6
- out_proj: bfloat16 [640, 1280], replicated, may hold values from -0.25 to 0.25
Outputs:
- grad_queries: bfloat16 [16, 8192, 640], P('dp', 'ctx')
- grad_keys: bfloat16 [16, 8192, 640], P('dp', 'ctx')
- grad_values: bfloat16 [16, 8192, 640], P('dp', 'ctx')
- grad_out_proj: float32 [1280, 640], P(('dp', 'ctx'))
The draws below stay inside these ranges and needn't reach their ends.
All inputs are finite; a program needn't handle non-finite values.
Results may differ from the reference program's by a relative error of at most 0.028.
Values may be sent and summed in bfloat16 or wider, within the bound.
No kernel may reach another device: no remote copies, remote signals or barrier semaphores. Data moves between devices by JAX's collectives and lax.ppermute only.
A program may use at most 64 MiB of HBM per device.

```python
import jax
import jax.numpy as jnp
from jax import lax

D = 1280
HEADS = 10
HDIM = 64
REACH = 2
TOK_DEV = 512
HD = 640
BATCH = 16
SEQ = 8192
TOKENS = 131072


def draw_queries(key, part):
    key = jax.random.fold_in(key, 11)
    base = jnp.clip(2.0 * jax.random.normal(key, (BATCH, SEQ, HD), jnp.float32), -6.0, 6.0)
    return base.astype(jnp.bfloat16)


def draw_keys(key, part):
    key = jax.random.fold_in(key, 13)
    base = jnp.clip(jax.random.normal(key, (BATCH, SEQ, HD), jnp.float32), -6.0, 6.0)
    return base.astype(jnp.bfloat16)


def block_scale(key, extent, cuts, smallest, high):
    gain = 1.0
    for dim, parts in cuts:
        draws = jax.random.uniform(jax.random.fold_in(jax.random.fold_in(key, 6), dim), (parts,), jnp.float32, smallest / len(cuts), high / len(cuts))
        gain = gain * jnp.repeat(jnp.exp(draws), extent[dim] // parts).reshape((-1,) + (1,) * (len(extent) - 1 - dim))
    return gain


def scatter_about(own_key, extent, scale, reach, pieces=(), held_as=jnp.bfloat16):
    factor_of = block_scale(own_key, extent, pieces, -0.22, 0.18) if pieces else 1.0
    values = jax.random.normal(own_key, extent, jnp.float32) * scale * factor_of
    return jnp.minimum(jnp.maximum(values, -reach), reach).astype(held_as)


def setup_inputs(seed: int = 0) -> dict:
    seeds = jax.random.split(jax.random.key(seed), 6)
    return {
        "queries": draw_queries(jax.random.fold_in(seeds[5], 71), 0),
        "keys": draw_keys(jax.random.fold_in(seeds[5], 71), 0),
        "values": scatter_about(seeds[2], (BATCH, SEQ, HD), 4.0, 16.0, ((0, 16), (1, 16))),
        "grad_out": scatter_about(seeds[3], (BATCH, SEQ, D), 1.0, 6.0, ((0, 16), (1, 16))),
        "out_proj": scatter_about(seeds[4], (HD, D), HD ** -0.5, 0.25),
    }


def block_grads(qb, kw, vw, gb, valid):
    tok = qb.shape[0]
    scale = HDIM ** -0.5
    qh = qb.reshape(tok, HEADS, HDIM).astype(jnp.float32)
    kh = kw.reshape(-1, HEADS, HDIM).astype(jnp.float32)
    vh = vw.reshape(-1, HEADS, HDIM).astype(jnp.float32)
    gh = gb.reshape(tok, HEADS, HDIM).astype(jnp.float32)
    key_mask = jnp.repeat(valid, tok)
    scores = jnp.einsum("qhd,khd->hqk", qh, kh) * scale
    scores = jnp.where(key_mask[None, None, :], scores, -jnp.inf)
    top = jnp.max(scores, axis=-1, keepdims=True)
    lse = top + jnp.log(jnp.sum(jnp.exp(scores - top), axis=-1, keepdims=True))
    probs = jnp.exp(scores - lse)
    probs_b = probs.astype(jnp.bfloat16).astype(jnp.float32)
    attn = jnp.einsum("hqk,khd->qhd", probs_b, vh).astype(jnp.bfloat16)
    attn_f = attn.astype(jnp.float32)
    delta = jnp.sum(gh * attn_f, axis=-1).T[:, :, None]
    dprob = jnp.einsum("qhd,khd->hqk", gh, vh)
    dscore = (probs * (dprob - delta)).astype(jnp.bfloat16).astype(jnp.float32)
    grad_q = (jnp.einsum("hqk,khd->qhd", dscore, kh) * scale).astype(jnp.bfloat16)
    part_k = (jnp.einsum("hqk,qhd->khd", dscore, qh) * scale).astype(jnp.bfloat16)
    part_v = jnp.einsum("hqk,qhd->khd", probs_b, gh).astype(jnp.bfloat16)
    width = 2 * REACH + 1
    return (grad_q.reshape(tok, -1), part_k.reshape(width, tok, -1),
            part_v.reshape(width, tok, -1), attn.reshape(tok, -1))


def one_recording(args):
    q, k, v, dy, out_proj = args
    blocks = SEQ // TOK_DEV
    grad_attn = lax.dot_general(dy, out_proj, (((1,), (1,)), ((), ())),
                                preferred_element_type=jnp.float32).astype(jnp.bfloat16)
    pad = jnp.zeros((REACH * TOK_DEV, q.shape[1]), q.dtype)
    kp = jnp.concatenate([pad, k, pad], axis=0)
    vp = jnp.concatenate([pad, v, pad], axis=0)
    offsets = jnp.arange(-REACH, REACH + 1, dtype=jnp.int32)

    def per_block(i):
        start = (i * TOK_DEV).astype(jnp.int32)
        kw = lax.dynamic_slice_in_dim(kp, start, (2 * REACH + 1) * TOK_DEV, 0)
        vw = lax.dynamic_slice_in_dim(vp, start, (2 * REACH + 1) * TOK_DEV, 0)
        qb = lax.dynamic_slice_in_dim(q, start, TOK_DEV, 0)
        gb = lax.dynamic_slice_in_dim(grad_attn, start, TOK_DEV, 0)
        valid = (i + offsets >= 0) & (i + offsets < blocks)
        return block_grads(qb, kw, vw, gb, valid)

    gq, pk, pv, attn = lax.map(per_block, jnp.arange(blocks, dtype=jnp.int32))
    zeros = jnp.zeros((REACH,) + pk.shape[1:], pk.dtype)
    pk = jnp.concatenate([zeros, pk, zeros], axis=0)
    pv = jnp.concatenate([zeros, pv, zeros], axis=0)
    gk = jnp.zeros((blocks,) + pk.shape[2:], jnp.float32)
    gv = jnp.zeros((blocks,) + pk.shape[2:], jnp.float32)
    for off in range(-REACH, REACH + 1):
        lo = REACH - off
        gk = gk + pk[lo:lo + blocks, off + REACH].astype(jnp.float32)
        gv = gv + pv[lo:lo + blocks, off + REACH].astype(jnp.float32)
    attn = attn.reshape(SEQ, -1)
    proj = lax.dot_general(dy, attn, (((0,), (0,)), ((), ())), preferred_element_type=jnp.float32)
    return (gq.reshape(SEQ, -1), gk.astype(jnp.bfloat16).reshape(SEQ, -1),
            gv.astype(jnp.bfloat16).reshape(SEQ, -1), proj)


def reference(queries, keys, values, grad_out, out_proj):
    def per_rec(b):
        return one_recording((queries[b], keys[b], values[b], grad_out[b], out_proj))

    gq, gk, gv, proj = lax.map(per_rec, jnp.arange(queries.shape[0], dtype=jnp.int32))
    total = jnp.sum(proj, axis=0) * (TOKENS ** -0.5)
    return gq, gk, gv, total
```

```python
import jax
import jax.numpy as jnp
from jax import lax
from jax.sharding import PartitionSpec as P

HEADS = 10
HDIM = 64
REACH = 2


def passed_along(x, axis, by):
    devices = lax.axis_size(axis)
    pairs = [(i, i + by) for i in range(devices) if 0 <= i + by < devices]
    return lax.ppermute(x, axis, pairs)


def shards(queries, keys, values, grad_out, out_proj):
    tok = queries.shape[1]
    width = 2 * REACH + 1
    scale = HDIM ** (-0.5)
    index = lax.axis_index("ctx")
    blocks = lax.axis_size("ctx")
    q_loc = queries[0]
    k_loc = keys[0]
    v_loc = values[0]
    dy_loc = grad_out[0]
    grad_attn = lax.dot_general(
        dy_loc, out_proj, (((1,), (1,)), ((), ())), preferred_element_type=jnp.float32
    ).astype(jnp.bfloat16)
    nearby = {0: (k_loc, v_loc)}
    for offset in (-2, -1, 1, 2):
        nearby[offset] = passed_along((k_loc, v_loc), "ctx", -offset)
    order = list(range(-REACH, REACH + 1))
    key_all = jnp.concatenate([nearby[o][0] for o in order], axis=0)
    val_all = jnp.concatenate([nearby[o][1] for o in order], axis=0)
    valid = jnp.stack([(index + o >= 0) & (index + o < blocks) for o in order])
    key_mask = jnp.repeat(valid, tok)
    q_heads = q_loc.reshape(tok, HEADS, HDIM).transpose(1, 0, 2)
    k_heads = key_all.reshape(width * tok, HEADS, HDIM).transpose(1, 0, 2)
    v_heads = val_all.reshape(width * tok, HEADS, HDIM).transpose(1, 0, 2)
    g_heads = grad_attn.reshape(tok, HEADS, HDIM).transpose(1, 0, 2)

    def head_grads(inputs):
        q_one, k_one, v_one, g_one = inputs
        scores = (
            lax.dot_general(
                q_one, k_one, (((1,), (1,)), ((), ())), preferred_element_type=jnp.float32
            )
            * scale
        )
        scores = jnp.where(key_mask[None, :], scores, -jnp.inf)
        top = jnp.max(scores, axis=-1, keepdims=True)
        lse = top + jnp.log(jnp.sum(jnp.exp(scores - top), axis=-1, keepdims=True))
        probs = jnp.exp(scores - lse)
        probs_b = probs.astype(jnp.bfloat16)
        attn_one = jnp.dot(probs_b, v_one, preferred_element_type=jnp.float32).astype(jnp.bfloat16)
        delta = jnp.sum(
            g_one.astype(jnp.float32) * attn_one.astype(jnp.float32), axis=-1, keepdims=True
        )
        dprob = lax.dot_general(
            g_one, v_one, (((1,), (1,)), ((), ())), preferred_element_type=jnp.float32
        )
        dscore = (probs * (dprob - delta)).astype(jnp.bfloat16)
        gq_one = (jnp.dot(dscore, k_one, preferred_element_type=jnp.float32) * scale).astype(
            jnp.bfloat16
        )
        pk_one = (
            lax.dot_general(
                dscore, q_one, (((0,), (0,)), ((), ())), preferred_element_type=jnp.float32
            )
            * scale
        ).astype(jnp.bfloat16)
        pv_one = lax.dot_general(
            probs_b, g_one, (((0,), (0,)), ((), ())), preferred_element_type=jnp.float32
        ).astype(jnp.bfloat16)
        return (gq_one, pk_one, pv_one, attn_one)

    grad_q, part_k, part_v, attn = lax.map(head_grads, (q_heads, k_heads, v_heads, g_heads))
    grad_q = grad_q.transpose(1, 0, 2).reshape(tok, -1)
    attn = attn.transpose(1, 0, 2)
    part_k = part_k.transpose(1, 0, 2).reshape(width, tok, -1)
    part_v = part_v.transpose(1, 0, 2).reshape(width, tok, -1)
    total_k = part_k[REACH].astype(jnp.float32)
    total_v = part_v[REACH].astype(jnp.float32)
    for offset in (-2, -1, 1, 2):
        got = passed_along((part_k[offset + REACH], part_v[offset + REACH]), "ctx", offset)
        total_k = total_k + got[0].astype(jnp.float32)
        total_v = total_v + got[1].astype(jnp.float32)
    attn_flat = attn.reshape(tok, -1)
    norm = float(tok * blocks * lax.axis_size("dp")) ** (-0.5)
    term = lax.dot_general(
        dy_loc, attn_flat, (((0,), (0,)), ((), ())), preferred_element_type=jnp.float32
    )
    term = (term * norm).astype(jnp.bfloat16)
    dps = lax.axis_size("dp")
    term = term.reshape(dps, -1, term.shape[1])
    term = lax.all_to_all(term, "dp", 0, 0)
    term = jnp.sum(term.astype(jnp.float32), axis=0)
    term = term.reshape(blocks, -1, term.shape[1])
    term = lax.all_to_all(term, "ctx", 0, 0)
    proj = jnp.sum(term, axis=0)
    return (
        grad_q.reshape(1, tok, -1),
        total_k.astype(jnp.bfloat16)[None],
        total_v.astype(jnp.bfloat16)[None],
        proj,
    )


def solution(mesh):
    in_specs = (
        P("dp", "ctx", None),
        P("dp", "ctx", None),
        P("dp", "ctx", None),
        P("dp", "ctx", None),
        P(),
    )
    out_specs = (
        P("dp", "ctx", None),
        P("dp", "ctx", None),
        P("dp", "ctx", None),
        P(("dp", "ctx"), None),
    )
    return jax.shard_map(shards, mesh=mesh, in_specs=in_specs, out_specs=out_specs, check_vma=False)
```

```python
import functools
import math

import jax
import jax.numpy as jnp
from jax import lax
from jax.experimental import pallas as pl
from jax.experimental.pallas import tpu as pltpu
from jax.sharding import PartitionSpec as P

HEADS = 10
HDIM = 64
HALF = HEADS // 2
ROWS = HALF * HDIM
TOK = 512
SCALE = HDIM ** (-0.5)
BASE2 = SCALE * math.log2(math.e)
BIG = 1e30
F32 = jnp.float32
BF16 = jnp.bfloat16

UNSEEN = ((5,), (0,))


def params(us):
    return dict(
        compiler_params=pltpu.CompilerParams(vmem_limit_bytes=60 * 2**20),
        cost_estimate=pl.CostEstimate(
            flops=int(us * 1.15e9), bytes_accessed=int(us * 1e5), transcendentals=0
        ),
    )


def mm(a, b, ca, cb):
    return lax.dot_general(a, b, (((ca,), (cb,)), ((), ())), preferred_element_type=F32)


def head_block(parts):
    return pl.BlockSpec((parts, HDIM, TOK), lambda h, s: (0, h, 0))


LSE_BLOCK = pl.BlockSpec((1, 2, TOK), lambda h, s: (h, 0, 0))


def head_major(parts, dtype=BF16):
    return jax.ShapeDtypeStruct((parts, ROWS, TOK), dtype)


def whole(shape):
    return pl.BlockSpec(shape, lambda i, s: (0,) * len(shape))


def halves(x):
    return x[:ROWS], x[ROWS:]


def in_order(odd, mine, partners):
    first = jnp.where(odd, partners, mine)
    return jnp.concatenate([first, jnp.where(odd, mine, partners)], axis=0)


def split_kernel(scal, a_ref, b_ref, mine, send):
    odd = scal[2] > 0
    for n, ref in enumerate((a_ref, b_ref)):
        low, high = halves(jnp.transpose(ref[...]))
        mine[n] = jnp.where(odd, high, low)
        send[n] = jnp.where(odd, low, high)


def split_heads(scal, a, b):
    return pl.pallas_call(
        split_kernel,
        grid_spec=pltpu.PrefetchScalarGridSpec(
            num_scalar_prefetch=1,
            grid=(1,),
            in_specs=[whole(a.shape)] * 2,
            out_specs=[whole((2, ROWS, TOK))] * 2,
        ),
        out_shape=[head_major(2)] * 2,
        name="split_kv",
        **params(3),
    )(scal, a, b)


def split_q_kernel(scal, q_ref, dy_ref, w_ref, mine, send):
    odd = scal[2] > 0
    grad = mm(w_ref[...], dy_ref[...], 1, 1).astype(BF16)
    for n, turned in enumerate((jnp.transpose(q_ref[...]), grad)):
        low, high = halves(turned)
        mine[n] = jnp.where(odd, high, low)
        send[n] = jnp.where(odd, low, high)


def split_queries(scal, q, dy, w):
    return pl.pallas_call(
        split_q_kernel,
        grid_spec=pltpu.PrefetchScalarGridSpec(
            num_scalar_prefetch=1,
            grid=(1,),
            in_specs=[whole(q.shape), whole(dy.shape), whole(w.shape)],
            out_specs=[whole((2, ROWS, TOK))] * 2,
        ),
        out_shape=[head_major(2)] * 2,
        name="split_q_and_grad",
        **params(5),
    )(scal, q, dy, w)


def side_flag(scal, j):
    return None if j in (2, 3) else scal[0] if j < 2 else scal[1]


def forward_kernel(scal, qm, qp, *refs):
    kv = refs[:6]
    om, op, lse = refs[6:]
    qs = (qm[0], qp[0])
    units = [(j, i) for j in (2, 3, 1, 4, 0, 5) for i in (0, 1) if j not in UNSEEN[i]]
    turned = {}

    def scores(j, i):
        if j not in turned:
            turned[j] = jnp.transpose(kv[j][0])
        return mm(turned[j], qs[i], 1, 0)

    top = [None, None]
    total = [None, None]
    out = [None, None]
    ahead = scores(*units[0])
    for n, (j, i) in enumerate(units):
        s = ahead
        if n + 1 < len(units):
            ahead = scores(*units[n + 1])
        flag = side_flag(scal, j)
        here = jnp.max(s, axis=0, keepdims=True) * BASE2
        if flag is not None:
            here = jnp.where(flag > 0, here, -BIG)
        first = top[i] is None
        new = here if first else jnp.maximum(top[i], here)
        sub = new if flag is None else jnp.where(flag > 0, new, BIG)
        e = jnp.exp2(s * BASE2 - sub)
        part = jnp.sum(e, axis=0, keepdims=True)
        pv = mm(kv[j][1], e.astype(BF16), 1, 0)
        if first:
            total[i], out[i] = part, pv
        else:
            fade = jnp.exp2(top[i] - new)
            total[i] = total[i] * fade + part
            out[i] = out[i] * fade + pv
        top[i] = new
    for i, ref in ((0, om), (1, op)):
        ref[0] = (out[i] * (1.0 / total[i])).astype(BF16)
        lse[0, i : i + 1, :] = top[i] + jnp.log2(total[i])


def forward(scal, qg, kv):
    return pl.pallas_call(
        forward_kernel,
        grid_spec=pltpu.PrefetchScalarGridSpec(
            num_scalar_prefetch=1,
            grid=(HALF,),
            in_specs=[head_block(1)] * 2 + [head_block(2)] * 6,
            out_specs=[head_block(1)] * 2 + [LSE_BLOCK],
        ),
        out_shape=[head_major(1)] * 2 + [jax.ShapeDtypeStruct((HALF, 2, TOK), F32)],
        name="attention_and_lse",
        **params(20),
    )(scal, *qg, *kv)


def backward_kernel(js, carry, last, scal, qgm, qgp, om, op, lse, *refs):
    n = len(js)
    kv, refs = refs[:n], refs[n:]
    if carry:
        dq_in, refs = refs[:2], refs[2:]
    dkv, dq_out = refs[:n], refs[n:]
    qs = (qgm[0], qgp[0])
    gs = (qgm[1], qgp[1])
    os = (om[0], op[0])
    ls = [lse[0, i : i + 1, :] for i in (0, 1)]
    delta = [
        jnp.sum(gs[i].astype(F32) * os[i].astype(F32), axis=0, keepdims=True) for i in (0, 1)
    ]
    q_turned = [jnp.transpose(x) for x in qs]
    g_turned = [jnp.transpose(x) for x in gs]
    dq = [dq_in[0][0], dq_in[1][0]] if carry else [None, None]
    for idx, j in enumerate(js):
        kt = kv[idx][0]
        k = jnp.transpose(kt)
        v = jnp.transpose(kv[idx][1])
        flag = side_flag(scal, j)
        dk = dv = None
        for i in (0, 1):
            if j in UNSEEN[i]:
                continue
            sub = ls[i] if flag is None else jnp.where(flag > 0, ls[i], BIG)
            p = jnp.exp2(mm(k, qs[i], 1, 0) * BASE2 - sub)
            ds = (p * (mm(v, gs[i], 1, 0) - delta[i])).astype(BF16)
            a = mm(p.astype(BF16), g_turned[i], 1, 0)
            b = mm(ds, q_turned[i], 1, 0)
            dv = a if dv is None else dv + a
            dk = b if dk is None else dk + b
            x = mm(kt, ds, 1, 0)
            dq[i] = x if dq[i] is None else dq[i] + x
        dkv[idx][0] = (jnp.transpose(dk) * SCALE).astype(dkv[idx].dtype)
        dkv[idx][1] = jnp.transpose(dv).astype(dkv[idx].dtype)
    for i in (0, 1):
        dq_out[i][0] = (dq[i] * SCALE).astype(BF16) if last else dq[i]


def backward(js, scal, qg, o, lse, kv, dq_in, last, dtypes, us):
    n = len(js)
    carry = dq_in is not None
    return pl.pallas_call(
        functools.partial(backward_kernel, js, carry, last),
        grid_spec=pltpu.PrefetchScalarGridSpec(
            num_scalar_prefetch=1,
            grid=(HALF,),
            in_specs=[head_block(2)] * 2
            + [head_block(1)] * 2
            + [LSE_BLOCK]
            + [head_block(2)] * n
            + [head_block(1)] * (2 if carry else 0),
            out_specs=[head_block(2)] * n + [head_block(1)] * 2,
        ),
        out_shape=[head_major(2, t) for t in dtypes]
        + [head_major(1, BF16 if last else F32)] * 2,
        name="backward_" + "".join(str(j) for j in js),
        **params(us),
    )(scal, *qg, *o, lse, *[kv[j] for j in js], *(dq_in if carry else ()))


def finish_kernel(scal, dq, dq_got, mid, a, b, got, gq, gk, gv):
    odd = scal[2] > 0
    gq[...] = jnp.transpose(in_order(odd, dq[0], dq_got[0]))
    for n, ref in ((0, gk), (1, gv)):
        total = mid[n] + a[n].astype(F32) + b[n].astype(F32)
        ref[...] = jnp.transpose(in_order(odd, total.astype(BF16), got[n]))


def finish(scal, dq, dq_got, mid, a, b, got):
    out = (TOK, 2 * ROWS)
    return pl.pallas_call(
        finish_kernel,
        grid_spec=pltpu.PrefetchScalarGridSpec(
            num_scalar_prefetch=1,
            grid=(1,),
            in_specs=[whole((1, ROWS, TOK))] * 2 + [whole((2, ROWS, TOK))] * 4,
            out_specs=[whole(out)] * 3,
        ),
        out_shape=[jax.ShapeDtypeStruct(out, BF16)] * 3,
        name="sum_and_turn",
        **params(4),
    )(scal, dq, dq_got, mid, a, b, got)


def project_kernel(norm, scal, o, o_got, dy, term):
    odd = scal[2] > 0
    attn = in_order(odd, o[0], o_got[0])
    turned = jnp.transpose(dy[...])
    term[...] = (mm(turned, attn, 1, 1) * norm).astype(BF16)


def project(scal, o, o_got, dy, norm):
    wide = 256
    return pl.pallas_call(
        functools.partial(project_kernel, norm),
        grid_spec=pltpu.PrefetchScalarGridSpec(
            num_scalar_prefetch=1,
            grid=(dy.shape[1] // wide,),
            in_specs=[whole((1, ROWS, TOK))] * 2
            + [pl.BlockSpec((TOK, wide), lambda i, s: (0, i))],
            out_specs=pl.BlockSpec((wide, 2 * ROWS), lambda i, s: (i, 0)),
        ),
        out_shape=jax.ShapeDtypeStruct((dy.shape[1], 2 * ROWS), BF16),
        name="projection_term",
        **params(4),
    )(scal, o, o_got, dy)


def shards(queries, keys, values, grad_out, out_proj):
    me = lax.axis_index("ctx")
    blocks = lax.axis_size("ctx")
    odd = me % 2
    below = (me >= 2).astype(jnp.int32)
    above = (me < blocks - 2).astype(jnp.int32)
    scal = jnp.stack(
        [jnp.where(odd == 0, below, above), jnp.where(odd == 0, above, below), odd]
    ).astype(jnp.int32)
    swap_pairs = [(i, i ^ 1) for i in range(blocks)]
    step_a = [(i, i + (2 if i % 2 == 0 else -2)) for i in range(blocks)]
    step_b = [(i, i - (2 if i % 2 == 0 else -2)) for i in range(blocks)]
    step_a = [(i, t) for i, t in step_a if 0 <= t < blocks]
    step_b = [(i, t) for i, t in step_b if 0 <= t < blocks]

    def swap(x):
        return lax.ppermute(x, "ctx", swap_pairs)

    def to_a(x):
        return lax.ppermute(x, "ctx", step_a)

    def to_b(x):
        return lax.ppermute(x, "ctx", step_b)

    dy = grad_out[0]
    kv_mine, kv_send = split_heads(scal, keys[0], values[0])
    kv_got = swap(kv_send)
    a_mine, b_mine = to_a(kv_mine), to_b(kv_mine)
    qg_mine, qg_send = split_queries(scal, queries[0], dy, out_proj)
    qg_got = swap(qg_send)
    a_got, b_got = to_a(kv_got), to_b(kv_got)
    kv = (a_mine, a_got, kv_mine, kv_got, b_mine, b_got)
    qg = (qg_mine, qg_got)
    o_mine, o_send, lse = forward(scal, qg, kv)
    o_got = swap(o_send)
    o = (o_mine, o_send)

    pa_p, pb_p, dq_m, dq_p = backward(
        (1, 5), scal, qg, o, lse, kv, None, False, (BF16, BF16), 13
    )
    back_a_p, back_b_p = to_b(pa_p), to_a(pb_p)
    pa_m, pb_m, mid_p, dq_m, dq_p = backward(
        (0, 4, 3), scal, qg, o, lse, kv, (dq_m, dq_p), False, (BF16, BF16, F32), 20
    )
    back_a_m, back_b_m = to_b(pa_m), to_a(pb_m)
    sum_p = (mid_p + back_a_p.astype(F32) + back_b_p.astype(F32)).astype(BF16)
    got_kv = swap(sum_p)
    mid_m, dq_m, dq_p = backward((2,), scal, qg, o, lse, kv, (dq_m, dq_p), True, (F32,), 9)
    dq_got = swap(dq_p)

    dps = lax.axis_size("dp")
    norm = float(TOK * blocks * dps) ** (-0.5)
    term = project(scal, o_mine, o_got, dy, norm)
    term = lax.all_to_all(term.reshape(dps, -1, term.shape[1]), "dp", 0, 0)
    term = jnp.sum(term.astype(F32), axis=0)
    term = lax.all_to_all(term.reshape(blocks, -1, term.shape[1]), "ctx", 0, 0)
    proj = jnp.sum(term, axis=0)

    gq, gk, gv = finish(scal, dq_m, dq_got, mid_m, back_a_m, back_b_m, got_kv)
    return gq[None], gk[None], gv[None], proj


def solution(mesh):
    rows = P("dp", "ctx", None)
    return jax.shard_map(
        shards,
        mesh=mesh,
        in_specs=(rows, rows, rows, rows, P()),
        out_specs=(rows, rows, rows, P(("dp", "ctx"), None)),
        check_vma=False,
    )
```

```python
import functools
import math

import jax
import jax.numpy as jnp
from jax import lax
from jax.experimental import pallas as pl
from jax.experimental.pallas import tpu as pltpu
from jax.sharding import PartitionSpec as P

HEADS = 10
HDIM = 64
HALF = HEADS // 2
ROWS = HALF * HDIM
TOK = 512
SCALE = HDIM ** (-0.5)
BASE2 = SCALE * math.log2(math.e)
BIG = 1e30
F32 = jnp.float32
BF16 = jnp.bfloat16

UNSEEN = ((5,), (0,))


def params(us):
    return dict(
        compiler_params=pltpu.CompilerParams(vmem_limit_bytes=63 * 2**20),
        cost_estimate=pl.CostEstimate(
            flops=int(us * 1.15e9), bytes_accessed=int(us * 1e5), transcendentals=0
        ),
    )


def mm(a, b, ca, cb):
    return lax.dot_general(a, b, (((ca,), (cb,)), ((), ())), preferred_element_type=F32)


def head_block(parts):
    return pl.BlockSpec((parts, HDIM, TOK), lambda h, s: (0, h, 0))


def head_major(parts, dtype=BF16):
    return jax.ShapeDtypeStruct((parts, ROWS, TOK), dtype)


def whole(shape):
    return pl.BlockSpec(shape, lambda i, s: (0,) * len(shape))


def halves(x):
    return x[:ROWS], x[ROWS:]


def in_order(odd, mine, partners):
    first = jnp.where(odd, partners, mine)
    return jnp.concatenate([first, jnp.where(odd, mine, partners)], axis=0)


def split_kernel(scal, k_ref, v_ref, q_ref, kv_mine, kv_send, q_mine, q_send):
    odd = scal[2] > 0
    for n, ref in enumerate((k_ref, v_ref)):
        low, high = halves(jnp.transpose(ref[...]))
        kv_mine[n] = jnp.where(odd, high, low)
        kv_send[n] = jnp.where(odd, low, high)
    low, high = halves(jnp.transpose(q_ref[...]))
    q_mine[0] = jnp.where(odd, high, low)
    q_send[0] = jnp.where(odd, low, high)


def split_heads(scal, k, v, q):
    return pl.pallas_call(
        split_kernel,
        grid_spec=pltpu.PrefetchScalarGridSpec(
            num_scalar_prefetch=1,
            grid=(1,),
            in_specs=[whole(k.shape)] * 3,
            out_specs=[whole((2, ROWS, TOK))] * 2 + [whole((1, ROWS, TOK))] * 2,
        ),
        out_shape=[head_major(2)] * 2 + [head_major(1)] * 2,
        name="split_kvq",
        **params(4),
    )(scal, k, v, q)


def grad_kernel(scal, dy_ref, w_ref, mine, send):
    odd = scal[2] > 0
    low, high = halves(mm(w_ref[...], dy_ref[...], 1, 1).astype(BF16))
    mine[0] = jnp.where(odd, high, low)
    send[0] = jnp.where(odd, low, high)


def attention_grad(scal, dy, w):
    return pl.pallas_call(
        grad_kernel,
        grid_spec=pltpu.PrefetchScalarGridSpec(
            num_scalar_prefetch=1,
            grid=(1,),
            in_specs=[whole(dy.shape), whole(w.shape)],
            out_specs=[whole((1, ROWS, TOK))] * 2,
        ),
        out_shape=[head_major(1)] * 2,
        name="attention_grad",
        **params(4),
    )(scal, dy, w)


def side_flag(scal, j):
    return None if j in (2, 3) else scal[0] if j < 2 else scal[1]


def forward_kernel(js, carry, last, scal, qm, qp, *refs):
    kv, refs = refs[: len(js)], refs[len(js) :]
    qs = (qm[0], qp[0])
    units = [(n, i) for n, j in enumerate(js) for i in (0, 1) if j not in UNSEEN[i]]
    turned = {}

    def scores(n, i):
        if n not in turned:
            turned[n] = jnp.transpose(kv[n][0])
        return mm(turned[n], qs[i], 1, 0)

    top = [None, None]
    total = [None, None]
    out = [None, None]
    if carry:
        stats, o_in, refs = refs[0], refs[1:3], refs[3:]
        for i in (0, 1):
            top[i] = stats[0, i : i + 1, :]
            total[i] = stats[0, 2 + i : 3 + i, :]
            out[i] = o_in[i][0]
    om, op, stats_out = refs
    ahead = scores(*units[0])
    for n, (b, i) in enumerate(units):
        s = ahead
        if n + 1 < len(units):
            ahead = scores(*units[n + 1])
        flag = side_flag(scal, js[b])
        here = jnp.max(s, axis=0, keepdims=True) * BASE2
        if flag is not None:
            here = jnp.where(flag > 0, here, -BIG)
        first = top[i] is None
        new = here if first else jnp.maximum(top[i], here)
        sub = new if flag is None else jnp.where(flag > 0, new, BIG)
        e = jnp.exp2(s * BASE2 - sub)
        part = jnp.sum(e, axis=0, keepdims=True)
        pv = mm(kv[b][1], e.astype(BF16), 1, 0)
        if first:
            total[i], out[i] = part, pv
        else:
            fade = jnp.exp2(top[i] - new)
            total[i] = total[i] * fade + part
            out[i] = out[i] * fade + pv
        top[i] = new
    for i, ref in ((0, om), (1, op)):
        if last:
            ref[0] = (out[i] * (1.0 / total[i])).astype(BF16)
            stats_out[0, i : i + 1, :] = top[i] + jnp.log2(total[i])
        else:
            ref[0] = out[i]
            stats_out[0, i : i + 1, :] = top[i]
            stats_out[0, 2 + i : 3 + i, :] = total[i]


def stat_block(rows):
    return pl.BlockSpec((1, rows, TOK), lambda h, s: (h, 0, 0))


def forward(js, scal, q, kv, carry, last, us):
    given = () if carry is None else carry
    rows = 2 if last else 4
    return pl.pallas_call(
        functools.partial(forward_kernel, js, bool(given), last),
        grid_spec=pltpu.PrefetchScalarGridSpec(
            num_scalar_prefetch=1,
            grid=(HALF,),
            in_specs=[head_block(1)] * 2
            + [head_block(2)] * len(js)
            + ([stat_block(4)] + [head_block(1)] * 2 if given else []),
            out_specs=[head_block(1)] * 2 + [stat_block(rows)],
        ),
        out_shape=[head_major(1, BF16 if last else F32)] * 2
        + [jax.ShapeDtypeStruct((HALF, rows, TOK), F32)],
        name="forward_" + "".join(str(j) for j in js),
        **params(us),
    )(scal, *q, *[kv[j] for j in js], *given)


def backward_kernel(js, carry, last, scal, qm, qp, gm, gp, om, op, lse, *refs):
    n = len(js)
    kv, refs = refs[:n], refs[n:]
    if carry:
        dq_in, refs = refs[:2], refs[2:]
    dkv, dq_out = refs[:n], refs[n:]
    qs = (qm[0], qp[0])
    gs = (gm[0], gp[0])
    os = (om[0], op[0])
    ls = [lse[0, i : i + 1, :] for i in (0, 1)]
    delta = [
        jnp.sum(gs[i].astype(F32) * os[i].astype(F32), axis=0, keepdims=True) for i in (0, 1)
    ]
    q_turned = [jnp.transpose(x) for x in qs]
    dq = [dq_in[0][0], dq_in[1][0]] if carry else [None, None]
    units = [(idx, i) for idx, j in enumerate(js) for i in (0, 1) if j not in UNSEEN[i]]
    turned = {}

    def products(idx, i):
        if idx not in turned:
            turned[idx] = (jnp.transpose(kv[idx][0]), jnp.transpose(kv[idx][1]))
        k, v = turned[idx]
        return mm(k, qs[i], 1, 0), mm(v, gs[i], 1, 0)

    ahead = products(*units[0])
    dk = dv = None
    for n, (idx, i) in enumerate(units):
        s, dp = ahead
        if n + 1 < len(units):
            ahead = products(*units[n + 1])
        flag = side_flag(scal, js[idx])
        sub = ls[i] if flag is None else jnp.where(flag > 0, ls[i], BIG)
        p = jnp.exp2(s * BASE2 - sub)
        ds = (p * (dp - delta[i])).astype(BF16)
        a = mm(gs[i], p.astype(BF16), 1, 1)
        b = mm(ds, q_turned[i], 1, 0)
        dv = a if dv is None else dv + a
        dk = b if dk is None else dk + b
        x = mm(kv[idx][0], ds, 1, 0)
        dq[i] = x if dq[i] is None else dq[i] + x
        if n + 1 == len(units) or units[n + 1][0] != idx:
            dkv[idx][0] = (jnp.transpose(dk) * SCALE).astype(dkv[idx].dtype)
            dkv[idx][1] = dv.astype(dkv[idx].dtype)
            dk = dv = None
    for i in (0, 1):
        dq_out[i][0] = (dq[i] * SCALE).astype(BF16) if last else dq[i]


def backward(js, scal, q, g, o, lse, kv, dq_in, last, dtypes, us):
    n = len(js)
    carry = dq_in is not None
    return pl.pallas_call(
        functools.partial(backward_kernel, js, carry, last),
        grid_spec=pltpu.PrefetchScalarGridSpec(
            num_scalar_prefetch=1,
            grid=(HALF,),
            in_specs=[head_block(1)] * 6
            + [stat_block(2)]
            + [head_block(2)] * n
            + [head_block(1)] * (2 if carry else 0),
            out_specs=[head_block(2)] * n + [head_block(1)] * 2,
        ),
        out_shape=[head_major(2, t) for t in dtypes]
        + [head_major(1, BF16 if last else F32)] * 2,
        name="backward_" + "".join(str(j) for j in js),
        **params(us),
    )(scal, *q, *g, *o, lse, *[kv[j] for j in js], *(dq_in if carry else ()))


def finish_kernel(scal, dq, dq_got, mid, a, b, got, gq, gk, gv):
    odd = scal[2] > 0
    gq[...] = jnp.transpose(in_order(odd, dq[0], dq_got[0]))
    for n, ref in ((0, gk), (1, gv)):
        total = mid[n] + a[n].astype(F32) + b[n].astype(F32)
        ref[...] = jnp.transpose(in_order(odd, total.astype(BF16), got[n]))


def finish(scal, dq, dq_got, mid, a, b, got):
    out = (TOK, 2 * ROWS)
    return pl.pallas_call(
        finish_kernel,
        grid_spec=pltpu.PrefetchScalarGridSpec(
            num_scalar_prefetch=1,
            grid=(1,),
            in_specs=[whole((1, ROWS, TOK))] * 2 + [whole((2, ROWS, TOK))] * 4,
            out_specs=[whole(out)] * 3,
        ),
        out_shape=[jax.ShapeDtypeStruct(out, BF16)] * 3,
        name="sum_and_turn",
        **params(4),
    )(scal, dq, dq_got, mid, a, b, got)


def project_kernel(norm, scal, o, o_got, dy, term):
    odd = scal[2] > 0
    attn = in_order(odd, o[0], o_got[0])
    turned = jnp.transpose(dy[...])
    term[...] = (mm(turned, attn, 1, 1) * norm).astype(BF16)


def project(scal, o, o_got, dy, norm):
    wide = 256
    return pl.pallas_call(
        functools.partial(project_kernel, norm),
        grid_spec=pltpu.PrefetchScalarGridSpec(
            num_scalar_prefetch=1,
            grid=(dy.shape[1] // wide,),
            in_specs=[whole((1, ROWS, TOK))] * 2
            + [pl.BlockSpec((TOK, wide), lambda i, s: (0, i))],
            out_specs=pl.BlockSpec((wide, 2 * ROWS), lambda i, s: (i, 0)),
        ),
        out_shape=jax.ShapeDtypeStruct((dy.shape[1], 2 * ROWS), BF16),
        name="projection_term",
        **params(4),
    )(scal, o, o_got, dy)


def shards(queries, keys, values, grad_out, out_proj):
    me = lax.axis_index("ctx")
    blocks = lax.axis_size("ctx")
    odd = me % 2
    below = (me >= 2).astype(jnp.int32)
    above = (me < blocks - 2).astype(jnp.int32)
    scal = jnp.stack(
        [jnp.where(odd == 0, below, above), jnp.where(odd == 0, above, below), odd]
    ).astype(jnp.int32)
    swap_pairs = [(i, i ^ 1) for i in range(blocks)]
    step_a = [(i, i + (2 if i % 2 == 0 else -2)) for i in range(blocks)]
    step_b = [(i, i - (2 if i % 2 == 0 else -2)) for i in range(blocks)]
    step_a = [(i, t) for i, t in step_a if 0 <= t < blocks]
    step_b = [(i, t) for i, t in step_b if 0 <= t < blocks]

    def swap(x):
        return lax.ppermute(x, "ctx", swap_pairs)

    def to_a(x):
        return lax.ppermute(x, "ctx", step_a)

    def to_b(x):
        return lax.ppermute(x, "ctx", step_b)

    dy = grad_out[0]
    kv_mine, kv_send, q_mine, q_send = split_heads(scal, keys[0], values[0], queries[0])
    kv_got = swap(kv_send)
    a_mine, b_mine = to_a(kv_mine), to_b(kv_mine)
    q_got = swap(q_send)
    g_mine, g_send = attention_grad(scal, dy, out_proj)
    g_got = swap(g_send)
    a_got, b_got = to_a(kv_got), to_b(kv_got)
    kv = (a_mine, a_got, kv_mine, kv_got, b_mine, b_got)
    q = (q_mine, q_got)
    g = (g_mine, g_got)
    early_m, early_p, stats = forward((2, 3, 4, 0), scal, q, kv, None, False, 16)
    o_mine, o_send, lse = forward((1, 5), scal, q, kv, (stats, early_m, early_p), True, 8)
    o_got = swap(o_send)
    o = (o_mine, o_send)

    pa_p, pb_p, dq_m, dq_p = backward(
        (1, 5), scal, q, g, o, lse, kv, None, False, (BF16, BF16), 13
    )
    back_a_p, back_b_p = to_b(pa_p), to_a(pb_p)
    pa_m, pb_m, mid_p, dq_m, dq_p = backward(
        (0, 4, 3), scal, q, g, o, lse, kv, (dq_m, dq_p), False, (BF16, BF16, F32), 20
    )
    back_a_m, back_b_m = to_b(pa_m), to_a(pb_m)
    sum_p = (mid_p + back_a_p.astype(F32) + back_b_p.astype(F32)).astype(BF16)
    got_kv = swap(sum_p)

    dps = lax.axis_size("dp")
    norm = float(TOK * blocks * dps) ** (-0.5)
    term = project(scal, o_mine, o_got, dy, norm)
    term = lax.all_to_all(term.reshape(dps, -1, term.shape[1]), "dp", 0, 0)
    term = jnp.sum(term.astype(F32), axis=0)
    term = term.reshape(blocks, -1, term.shape[1])
    term, dq_m = lax.optimization_barrier((term, dq_m))
    term = lax.all_to_all(term, "ctx", 0, 0)
    proj = jnp.sum(term, axis=0)

    mid_m, dq_m, dq_p = backward(
        (2,), scal, q, g, o, lse, kv, (dq_m, dq_p), True, (F32,), 9
    )
    dq_got = swap(dq_p)
    gq, gk, gv = finish(scal, dq_m, dq_got, mid_m, back_a_m, back_b_m, got_kv)
    return gq[None], gk[None], gv[None], proj


def solution(mesh):
    rows = P("dp", "ctx", None)
    return jax.shard_map(
        shards,
        mesh=mesh,
        in_specs=(rows, rows, rows, rows, P()),
        out_specs=(rows, rows, rows, P(("dp", "ctx"), None)),
        check_vma=False,
    )
```

```python
import functools
import math

import jax
import jax.numpy as jnp
from jax import lax
from jax.experimental import pallas as pl
from jax.experimental.pallas import tpu as pltpu
from jax.sharding import PartitionSpec as P

HEADS = 10
HDIM = 64
HALF = HEADS // 2
ROWS = HALF * HDIM
TOK = 512
SCALE = HDIM ** (-0.5)
BASE2 = SCALE * math.log2(math.e)
BIG = 1e30
F32 = jnp.float32
BF16 = jnp.bfloat16

UNSEEN = ((5,), (0,))


def params(us):
    return dict(
        compiler_params=pltpu.CompilerParams(vmem_limit_bytes=63 * 2**20),
        cost_estimate=pl.CostEstimate(
            flops=int(us * 1.15e9), bytes_accessed=int(us * 1e5), transcendentals=0
        ),
    )


def mm(a, b, ca, cb):
    return lax.dot_general(a, b, (((ca,), (cb,)), ((), ())), preferred_element_type=F32)


def head_block(parts):
    return pl.BlockSpec((parts, HDIM, TOK), lambda h, s: (0, h, 0))


def head_major(parts, dtype=BF16):
    return jax.ShapeDtypeStruct((parts, ROWS, TOK), dtype)


def whole(shape):
    return pl.BlockSpec(shape, lambda i, s: (0,) * len(shape))


def halves(x):
    return x[:ROWS], x[ROWS:]


def in_order(odd, mine, partners):
    first = jnp.where(odd, partners, mine)
    return jnp.concatenate([first, jnp.where(odd, mine, partners)], axis=0)


def split_kernel(scal, k_ref, v_ref, q_ref, kv_mine, kv_send, q_mine, q_send):
    odd = scal[2] > 0
    for n, ref in enumerate((k_ref, v_ref)):
        low, high = halves(jnp.transpose(ref[...]))
        kv_mine[n] = jnp.where(odd, high, low)
        kv_send[n] = jnp.where(odd, low, high)
    low, high = halves(jnp.transpose(q_ref[...]))
    q_mine[0] = jnp.where(odd, high, low)
    q_send[0] = jnp.where(odd, low, high)


def split_heads(scal, k, v, q):
    return pl.pallas_call(
        split_kernel,
        grid_spec=pltpu.PrefetchScalarGridSpec(
            num_scalar_prefetch=1,
            grid=(1,),
            in_specs=[whole(k.shape)] * 3,
            out_specs=[whole((2, ROWS, TOK))] * 2 + [whole((1, ROWS, TOK))] * 2,
        ),
        out_shape=[head_major(2)] * 2 + [head_major(1)] * 2,
        name="split_kvq",
        **params(4),
    )(scal, k, v, q)


def grad_kernel(scal, dy_ref, w_ref, mine, send, dy_turned):
    odd = scal[2] > 0
    low, high = halves(mm(w_ref[...], dy_ref[...], 1, 1).astype(BF16))
    mine[0] = jnp.where(odd, high, low)
    send[0] = jnp.where(odd, low, high)
    dy_turned[...] = jnp.transpose(dy_ref[...])


def attention_grad(scal, dy, w):
    return pl.pallas_call(
        grad_kernel,
        grid_spec=pltpu.PrefetchScalarGridSpec(
            num_scalar_prefetch=1,
            grid=(1,),
            in_specs=[whole(dy.shape), whole(w.shape)],
            out_specs=[whole((1, ROWS, TOK))] * 2 + [whole(dy.shape[::-1])],
        ),
        out_shape=[head_major(1)] * 2 + [jax.ShapeDtypeStruct(dy.shape[::-1], BF16)],
        name="attention_grad",
        **params(4),
    )(scal, dy, w)


def side_flag(scal, j):
    return None if j in (2, 3) else scal[0] if j < 2 else scal[1]


def forward_kernel(js, carry, last, scal, qm, qp, *refs):
    kv, refs = refs[: len(js)], refs[len(js) :]
    qs = (qm[0], qp[0])
    units = [(n, i) for n, j in enumerate(js) for i in (0, 1) if j not in UNSEEN[i]]
    turned = {}

    def scores(n, i):
        if n not in turned:
            turned[n] = jnp.transpose(kv[n][0])
        return mm(turned[n], qs[i], 1, 0)

    top = [None, None]
    total = [None, None]
    out = [None, None]
    if carry:
        stats, o_in, refs = refs[0], refs[1:3], refs[3:]
        for i in (0, 1):
            top[i] = stats[0, i : i + 1, :]
            total[i] = stats[0, 2 + i : 3 + i, :]
            out[i] = o_in[i][0]
    om, op, stats_out = refs
    ahead = scores(*units[0])
    for n, (b, i) in enumerate(units):
        s = ahead
        if n + 1 < len(units):
            ahead = scores(*units[n + 1])
        flag = side_flag(scal, js[b])
        here = jnp.max(s, axis=0, keepdims=True) * BASE2
        if flag is not None:
            here = jnp.where(flag > 0, here, -BIG)
        first = top[i] is None
        new = here if first else jnp.maximum(top[i], here)
        sub = new if flag is None else jnp.where(flag > 0, new, BIG)
        e = jnp.exp2(s * BASE2 - sub)
        part = jnp.sum(e, axis=0, keepdims=True)
        pv = mm(kv[b][1], e.astype(BF16), 1, 0)
        if first:
            total[i], out[i] = part, pv
        else:
            fade = jnp.exp2(top[i] - new)
            total[i] = total[i] * fade + part
            out[i] = out[i] * fade + pv
        top[i] = new
    for i, ref in ((0, om), (1, op)):
        if last:
            ref[0] = (out[i] * (1.0 / total[i])).astype(BF16)
            stats_out[0, i : i + 1, :] = top[i] + jnp.log2(total[i])
        else:
            ref[0] = out[i]
            stats_out[0, i : i + 1, :] = top[i]
            stats_out[0, 2 + i : 3 + i, :] = total[i]


def stat_block(rows):
    return pl.BlockSpec((1, rows, TOK), lambda h, s: (h, 0, 0))


def forward(js, scal, q, kv, carry, last, us):
    given = () if carry is None else carry
    rows = 2 if last else 4
    return pl.pallas_call(
        functools.partial(forward_kernel, js, bool(given), last),
        grid_spec=pltpu.PrefetchScalarGridSpec(
            num_scalar_prefetch=1,
            grid=(HALF,),
            in_specs=[head_block(1)] * 2
            + [head_block(2)] * len(js)
            + ([stat_block(4)] + [head_block(1)] * 2 if given else []),
            out_specs=[head_block(1)] * 2 + [stat_block(rows)],
        ),
        out_shape=[head_major(1, BF16 if last else F32)] * 2
        + [jax.ShapeDtypeStruct((HALF, rows, TOK), F32)],
        name="forward_" + "".join(str(j) for j in js),
        **params(us),
    )(scal, *q, *[kv[j] for j in js], *given)


def backward_kernel(js, late, scal, qm, qp, gm, gp, om, op, lse, *refs):
    n = len(js)
    kv, refs = refs[:n], refs[n:]
    if late:
        dq_in, arrived, refs = refs[:2], refs[2:4], refs[4:]
    dkv, dq_out = refs[:n], refs[n:]
    qs = (qm[0], qp[0])
    gs = (gm[0], gp[0])
    os = (om[0], op[0])
    ls = [lse[0, i : i + 1, :] for i in (0, 1)]
    delta = [
        jnp.sum(gs[i].astype(F32) * os[i].astype(F32), axis=0, keepdims=True) for i in (0, 1)
    ]
    q_turned = [jnp.transpose(x) for x in qs]
    dq = [dq_in[0][0], dq_in[1][0]] if late else [None, None]
    units = [(idx, i) for idx, j in enumerate(js) for i in (0, 1) if j not in UNSEEN[i]]
    turned = {}

    def products(idx, i):
        if idx not in turned:
            turned[idx] = (jnp.transpose(kv[idx][0]), jnp.transpose(kv[idx][1]))
        k, v = turned[idx]
        return mm(k, qs[i], 1, 0), mm(v, gs[i], 1, 0)

    ahead = products(*units[0])
    dk = dv = None
    for n, (idx, i) in enumerate(units):
        s, dp = ahead
        if n + 1 < len(units):
            ahead = products(*units[n + 1])
        flag = side_flag(scal, js[idx])
        sub = ls[i] if flag is None else jnp.where(flag > 0, ls[i], BIG)
        p = jnp.exp2(s * BASE2 - sub)
        ds = (p * (dp - delta[i])).astype(BF16)
        a = mm(gs[i], p.astype(BF16), 1, 1)
        b = mm(ds, q_turned[i], 1, 0)
        dv = a if dv is None else dv + a
        dk = b if dk is None else dk + b
        x = mm(kv[idx][0], ds, 1, 0)
        dq[i] = x if dq[i] is None else dq[i] + x
        if n + 1 == len(units) or units[n + 1][0] != idx:
            dk = jnp.transpose(dk) * SCALE
            if late and js[idx] == 3:
                dk = dk + arrived[0][0].astype(F32) + arrived[1][0].astype(F32)
                dv = dv + arrived[0][1].astype(F32) + arrived[1][1].astype(F32)
            dkv[idx][0] = dk.astype(dkv[idx].dtype)
            dkv[idx][1] = dv.astype(dkv[idx].dtype)
            dk = dv = None
    if late:
        dq_out[0][0] = (dq[0] * SCALE).astype(BF16)
        dkv[js.index(3)][2] = (dq[1] * SCALE).astype(BF16)
    else:
        dq_out[0][0] = dq[0]
        dq_out[1][0] = dq[1]


def backward(js, scal, q, g, o, lse, kv, outs, dq_in=(), arrived=(), us=13):
    late = bool(arrived)
    dq_out = [head_major(1, BF16)] if late else [head_major(1, F32)] * 2
    return pl.pallas_call(
        functools.partial(backward_kernel, js, late),
        grid_spec=pltpu.PrefetchScalarGridSpec(
            num_scalar_prefetch=1,
            grid=(HALF,),
            in_specs=[head_block(1)] * 6
            + [stat_block(2)]
            + [head_block(2)] * len(js)
            + [head_block(1)] * len(dq_in)
            + [head_block(2)] * len(arrived),
            out_specs=[head_block(x.shape[0]) for x in outs]
            + [head_block(1)] * len(dq_out),
        ),
        out_shape=list(outs) + dq_out,
        name="backward_" + "".join(str(j) for j in js),
        **params(us),
    )(scal, *q, *g, *o, lse, *[kv[j] for j in js], *dq_in, *arrived)


def finish_kernel(scal, dq, mid, a, b, got, gq, gk, gv):
    odd = scal[2] > 0
    gq[...] = jnp.transpose(in_order(odd, dq[0], got[2]))
    for n, ref in ((0, gk), (1, gv)):
        total = mid[n] + a[n].astype(F32) + b[n].astype(F32)
        ref[...] = jnp.transpose(in_order(odd, total.astype(BF16), got[n]))


def finish(scal, dq, mid, a, b, got):
    out = (TOK, 2 * ROWS)
    return pl.pallas_call(
        finish_kernel,
        grid_spec=pltpu.PrefetchScalarGridSpec(
            num_scalar_prefetch=1,
            grid=(1,),
            in_specs=[whole((1, ROWS, TOK))]
            + [whole((2, ROWS, TOK))] * 3
            + [whole((3, ROWS, TOK))],
            out_specs=[whole(out)] * 3,
        ),
        out_shape=[jax.ShapeDtypeStruct(out, BF16)] * 3,
        name="sum_and_turn",
        **params(4),
    )(scal, dq, mid, a, b, got)


def project_kernel(norm, scal, o, o_got, dy_turned, term):
    attn = in_order(scal[2] > 0, o[0], o_got[0])
    term[...] = (mm(dy_turned[...], attn, 1, 1) * norm).astype(BF16)


def project(scal, o, o_got, dy_turned, norm):
    out = (dy_turned.shape[0], 2 * ROWS)
    return pl.pallas_call(
        functools.partial(project_kernel, norm),
        grid_spec=pltpu.PrefetchScalarGridSpec(
            num_scalar_prefetch=1,
            grid=(1,),
            in_specs=[whole((1, ROWS, TOK))] * 2 + [whole(dy_turned.shape)],
            out_specs=whole(out),
        ),
        out_shape=jax.ShapeDtypeStruct(out, BF16),
        name="projection_term",
        **params(4),
    )(scal, o, o_got, dy_turned)


def shards(queries, keys, values, grad_out, out_proj):
    me = lax.axis_index("ctx")
    blocks = lax.axis_size("ctx")
    odd = me % 2
    below = (me >= 2).astype(jnp.int32)
    above = (me < blocks - 2).astype(jnp.int32)
    scal = jnp.stack(
        [jnp.where(odd == 0, below, above), jnp.where(odd == 0, above, below), odd]
    ).astype(jnp.int32)
    swap_pairs = [(i, i ^ 1) for i in range(blocks)]
    step_a = [(i, i + (2 if i % 2 == 0 else -2)) for i in range(blocks)]
    step_b = [(i, i - (2 if i % 2 == 0 else -2)) for i in range(blocks)]
    step_a = [(i, t) for i, t in step_a if 0 <= t < blocks]
    step_b = [(i, t) for i, t in step_b if 0 <= t < blocks]

    def swap(x):
        return lax.ppermute(x, "ctx", swap_pairs)

    def to_a(x):
        return lax.ppermute(x, "ctx", step_a)

    def to_b(x):
        return lax.ppermute(x, "ctx", step_b)

    dy = grad_out[0]
    kv_mine, kv_send, q_mine, q_send = split_heads(scal, keys[0], values[0], queries[0])
    kv_got = swap(kv_send)
    a_mine, b_mine = to_a(kv_mine), to_b(kv_mine)
    q_got = swap(q_send)
    g_mine, g_send, dy_turned = attention_grad(scal, dy, out_proj)
    g_got = swap(g_send)
    a_got, b_got = to_a(kv_got), to_b(kv_got)
    kv = (a_mine, a_got, kv_mine, kv_got, b_mine, b_got)
    q = (q_mine, q_got)
    g = (g_mine, g_got)
    early_m, early_p, stats = forward((2, 3, 4, 0), scal, q, kv, None, False, 16)
    o_mine, o_send, lse = forward((1, 5), scal, q, kv, (stats, early_m, early_p), True, 8)
    o_got = swap(o_send)
    o = (o_mine, o_send)

    pair = head_major(2)
    pa, pb, dq_m, dq_p = backward((1, 5), scal, q, g, o, lse, kv, (pair, pair))
    arrived = (to_b(pa), to_a(pb))
    outs = (head_major(3), pair, pair, head_major(2, F32))
    for_partner, pa, pb, mid, dq = backward(
        (3, 0, 4, 2), scal, q, g, o, lse, kv, outs, (dq_m, dq_p), arrived, 27
    )
    got = swap(for_partner)
    back_a, back_b = to_b(pa), to_a(pb)

    dps = lax.axis_size("dp")
    norm = float(TOK * blocks * dps) ** (-0.5)
    term = project(scal, o_mine, o_got, dy_turned, norm)
    term = lax.all_to_all(term.reshape(dps, -1, term.shape[1]), "dp", 0, 0)
    term = jnp.sum(term.astype(F32), axis=0)
    term = term.reshape(blocks, -1, term.shape[1])
    term = lax.all_to_all(term, "ctx", 0, 0)
    proj = jnp.sum(term, axis=0)

    gq, gk, gv = finish(scal, dq, mid, back_a, back_b, got)
    return gq[None], gk[None], gv[None], proj


def solution(mesh):
    rows = P("dp", "ctx", None)
    return jax.shard_map(
        shards,
        mesh=mesh,
        in_specs=(rows, rows, rows, rows, P()),
        out_specs=(rows, rows, rows, P(("dp", "ctx"), None)),
        check_vma=False,
    )
```

```python
import functools
import math

import jax
import jax.numpy as jnp
from jax import lax
from jax.experimental import pallas as pl
from jax.experimental.pallas import tpu as pltpu
from jax.sharding import PartitionSpec as P

HEADS = 10
HDIM = 64
HALF = HEADS // 2
ROWS = HALF * HDIM
TOK = 512
SCALE = HDIM ** (-0.5)
BASE2 = SCALE * math.log2(math.e)
BIG = 1e30
FAR = 48.0
F32 = jnp.float32
BF16 = jnp.bfloat16

UNSEEN = ((5,), (0,))


def params(us):
    return dict(
        compiler_params=pltpu.CompilerParams(vmem_limit_bytes=63 * 2**20),
        cost_estimate=pl.CostEstimate(
            flops=int(us * 1.15e9), bytes_accessed=int(us * 1e5), transcendentals=0
        ),
    )


def mm(a, b, ca, cb):
    return lax.dot_general(a, b, (((ca,), (cb,)), ((), ())), preferred_element_type=F32)


def head_block(parts):
    return pl.BlockSpec((parts, HDIM, TOK), lambda h, s: (0, h, 0))


def head_major(parts, dtype=BF16):
    return jax.ShapeDtypeStruct((parts, ROWS, TOK), dtype)


def whole(shape):
    return pl.BlockSpec(shape, lambda i, s: (0,) * len(shape))


def halves(x):
    return x[:ROWS], x[ROWS:]


def in_order(odd, mine, partners):
    first = jnp.where(odd, partners, mine)
    return jnp.concatenate([first, jnp.where(odd, mine, partners)], axis=0)


def split_kernel(scal, k_ref, v_ref, q_ref, kv_mine, kv_send, q_mine, q_send):
    odd = scal[2] > 0
    for n, ref in enumerate((k_ref, v_ref)):
        low, high = halves(jnp.transpose(ref[...]))
        kv_mine[n] = jnp.where(odd, high, low)
        kv_send[n] = jnp.where(odd, low, high)
    low, high = halves(jnp.transpose(q_ref[...]))
    q_mine[0] = jnp.where(odd, high, low)
    q_send[0] = jnp.where(odd, low, high)


def split_heads(scal, k, v, q):
    return pl.pallas_call(
        split_kernel,
        grid_spec=pltpu.PrefetchScalarGridSpec(
            num_scalar_prefetch=1,
            grid=(1,),
            in_specs=[whole(k.shape)] * 3,
            out_specs=[whole((2, ROWS, TOK))] * 2 + [whole((1, ROWS, TOK))] * 2,
        ),
        out_shape=[head_major(2)] * 2 + [head_major(1)] * 2,
        name="split_kvq",
        **params(4),
    )(scal, k, v, q)


def grad_kernel(scal, dy_ref, w_ref, mine, send, dy_turned):
    odd = scal[2] > 0
    low, high = halves(mm(w_ref[...], dy_ref[...], 1, 1).astype(BF16))
    mine[0] = jnp.where(odd, high, low)
    send[0] = jnp.where(odd, low, high)
    dy_turned[...] = jnp.transpose(dy_ref[...])


def attention_grad(scal, dy, w):
    return pl.pallas_call(
        grad_kernel,
        grid_spec=pltpu.PrefetchScalarGridSpec(
            num_scalar_prefetch=1,
            grid=(1,),
            in_specs=[whole(dy.shape), whole(w.shape)],
            out_specs=[whole((1, ROWS, TOK))] * 2 + [whole(dy.shape[::-1])],
        ),
        out_shape=[head_major(1)] * 2 + [jax.ShapeDtypeStruct(dy.shape[::-1], BF16)],
        name="attention_grad",
        **params(4),
    )(scal, dy, w)


def side_flag(scal, j):
    return None if j in (2, 3) else scal[0] if j < 2 else scal[1]


def forward_kernel(js, carry, last, scal, qm, qp, *refs):
    kv, refs = refs[: len(js)], refs[len(js) :]
    qs = (qm[0], qp[0])
    units = [(n, i) for n, j in enumerate(js) for i in (0, 1) if j not in UNSEEN[i]]
    turned = {}

    def scores(n, i):
        if n not in turned:
            turned[n] = jnp.transpose(kv[n][0])
        return mm(turned[n], qs[i], 1, 0)

    if carry:
        stats, o_in, refs = refs[0], refs[1:3], refs[3:]
    om, op, stats_out = refs

    def run(running):
        top, total, out = [None, None], [None, None], [None, None]
        over = None
        if carry:
            for i in (0, 1):
                top[i] = stats[0, i : i + 1, :]
                total[i] = stats[0, 2 + i : 3 + i, :]
                out[i] = o_in[i][0]
        ahead = scores(*units[0])
        for n, (b, i) in enumerate(units):
            s = ahead
            if n + 1 < len(units):
                ahead = scores(*units[n + 1])
            flag = side_flag(scal, js[b])
            here = jnp.max(s, axis=0, keepdims=True) * BASE2
            if flag is not None:
                here = jnp.where(flag > 0, here, -BIG)
            first = top[i] is None
            if first:
                new = here
            elif running:
                new = jnp.maximum(top[i], here)
            else:
                new = top[i]
                over = here - new if over is None else jnp.maximum(over, here - new)
            sub = new if flag is None else jnp.where(flag > 0, new, BIG)
            e = jnp.exp2(s * BASE2 - sub)
            part = jnp.sum(e, axis=0, keepdims=True)
            pv = mm(kv[b][1], e.astype(BF16), 1, 0)
            if first:
                total[i], out[i] = part, pv
            elif running:
                fade = jnp.exp2(top[i] - new)
                total[i] = total[i] * fade + part
                out[i] = out[i] * fade + pv
            else:
                total[i] = total[i] + part
                out[i] = out[i] + pv
            top[i] = new
        for i, ref in ((0, om), (1, op)):
            if last:
                ref[0] = (out[i] * (1.0 / total[i])).astype(BF16)
                stats_out[0, i : i + 1, :] = top[i] + jnp.log2(total[i])
            else:
                ref[0] = out[i]
                stats_out[0, i : i + 1, :] = top[i]
                stats_out[0, 2 + i : 3 + i, :] = total[i]
        return over

    far = jnp.max(run(False)) > FAR

    @pl.when(far)
    def _():
        turned.clear()
        run(True)


def stat_block(rows):
    return pl.BlockSpec((1, rows, TOK), lambda h, s: (h, 0, 0))


def forward(js, scal, q, kv, carry, last, us):
    given = () if carry is None else carry
    rows = 2 if last else 4
    return pl.pallas_call(
        functools.partial(forward_kernel, js, bool(given), last),
        grid_spec=pltpu.PrefetchScalarGridSpec(
            num_scalar_prefetch=1,
            grid=(HALF,),
            in_specs=[head_block(1)] * 2
            + [head_block(2)] * len(js)
            + ([stat_block(4)] + [head_block(1)] * 2 if given else []),
            out_specs=[head_block(1)] * 2 + [stat_block(rows)],
        ),
        out_shape=[head_major(1, BF16 if last else F32)] * 2
        + [jax.ShapeDtypeStruct((HALF, rows, TOK), F32)],
        name="forward_" + "".join(str(j) for j in js),
        **params(us),
    )(scal, *q, *[kv[j] for j in js], *given)


def backward_kernel(js, pairs, stage, scal, qm, qp, gm, gp, om, op, lse, *refs):
    n = len(js)
    kv, refs = refs[:n], refs[n:]
    mine, partners = any(i == 0 for _, i in pairs), any(i == 1 for _, i in pairs)
    dq_in = ()
    if stage > 0:
        dq_in, refs = refs[: mine + partners], refs[mine + partners :]
    if stage == 1:
        arrived, refs = refs[:2], refs[2:]
    dkv, dq_out = refs[:n], refs[n:]
    qs = (qm[0], qp[0])
    gs = (gm[0], gp[0])
    os = (om[0], op[0])
    ls = [lse[0, i : i + 1, :] for i in (0, 1)]
    delta = [
        jnp.sum(gs[i].astype(F32) * os[i].astype(F32), axis=0, keepdims=True) for i in (0, 1)
    ]
    q_turned = [jnp.transpose(x) for x in qs]
    dq = [x[0] for x in dq_in] if stage > 0 else [None, None]
    units = [(js.index(j), i) for j, i in pairs]
    turned = {}

    def products(idx, i):
        if idx not in turned:
            turned[idx] = (jnp.transpose(kv[idx][0]), jnp.transpose(kv[idx][1]))
        k, v = turned[idx]
        return mm(k, qs[i], 1, 0), mm(v, gs[i], 1, 0)

    ahead = products(*units[0])
    dk = dv = None
    for n, (idx, i) in enumerate(units):
        s, dp = ahead
        if n + 1 < len(units):
            ahead = products(*units[n + 1])
        flag = side_flag(scal, js[idx])
        sub = ls[i] if flag is None else jnp.where(flag > 0, ls[i], BIG)
        p = jnp.exp2(s * BASE2 - sub)
        ds = (p * (dp - delta[i])).astype(BF16)
        a = mm(gs[i], p.astype(BF16), 1, 1)
        b = mm(ds, q_turned[i], 1, 0)
        dv = a if dv is None else dv + a
        dk = b if dk is None else dk + b
        x = mm(kv[idx][0], ds, 1, 0)
        dq[i] = x if dq[i] is None else dq[i] + x
        if n + 1 == len(units) or units[n + 1][0] != idx:
            dk = jnp.transpose(dk) * SCALE
            if stage == 1 and js[idx] == 3:
                dk = dk + arrived[0][0].astype(F32) + arrived[1][0].astype(F32)
                dv = dv + arrived[0][1].astype(F32) + arrived[1][1].astype(F32)
            dkv[idx][0] = dk.astype(dkv[idx].dtype)
            dkv[idx][1] = dv.astype(dkv[idx].dtype)
            dk = dv = None
    if stage == 0:
        dq_out[0][0] = dq[0]
        dq_out[1][0] = dq[1]
    elif stage == 1:
        dkv[js.index(3)][2] = (dq[1] * SCALE).astype(BF16)
        dq_out[0][0] = dq[0]
    else:
        dq_out[0][0] = (dq[0] * SCALE).astype(BF16)


def backward(stage, pairs, scal, q, g, o, lse, kv, outs, given=(), us=13):
    js = tuple(dict.fromkeys(j for j, _ in pairs))
    dq_out = [head_major(1, BF16 if stage == 2 else F32)] * (2 if stage == 0 else 1)
    return pl.pallas_call(
        functools.partial(backward_kernel, js, pairs, stage),
        grid_spec=pltpu.PrefetchScalarGridSpec(
            num_scalar_prefetch=1,
            grid=(HALF,),
            in_specs=[head_block(1)] * 6
            + [stat_block(2)]
            + [head_block(2)] * len(js)
            + [head_block(x.shape[0]) for x in given],
            out_specs=[head_block(x.shape[0]) for x in outs]
            + [head_block(1)] * len(dq_out),
        ),
        out_shape=list(outs) + dq_out,
        name="backward_" + "".join(str(j) for j in js),
        **params(us),
    )(scal, *q, *g, *o, lse, *[kv[j] for j in js], *given)


def finish_kernel(scal, dq, mid, rest, a, b, got, gq, gk, gv):
    odd = scal[2] > 0
    gq[...] = jnp.transpose(in_order(odd, dq[0], got[2]))
    for n, ref in ((0, gk), (1, gv)):
        total = mid[n] + rest[n] + a[n].astype(F32) + b[n].astype(F32)
        ref[...] = jnp.transpose(in_order(odd, total.astype(BF16), got[n]))


def finish(scal, dq, mid, rest, a, b, got):
    out = (TOK, 2 * ROWS)
    return pl.pallas_call(
        finish_kernel,
        grid_spec=pltpu.PrefetchScalarGridSpec(
            num_scalar_prefetch=1,
            grid=(1,),
            in_specs=[whole((1, ROWS, TOK))]
            + [whole((2, ROWS, TOK))] * 4
            + [whole((3, ROWS, TOK))],
            out_specs=[whole(out)] * 3,
        ),
        out_shape=[jax.ShapeDtypeStruct(out, BF16)] * 3,
        name="sum_and_turn",
        **params(4),
    )(scal, dq, mid, rest, a, b, got)


def project_kernel(norm, scal, o, o_got, dy_turned, term):
    attn = in_order(scal[2] > 0, o[0], o_got[0])
    term[...] = (mm(dy_turned[...], attn, 1, 1) * norm).astype(BF16)


def project(scal, o, o_got, dy_turned, norm):
    out = (dy_turned.shape[0], 2 * ROWS)
    return pl.pallas_call(
        functools.partial(project_kernel, norm),
        grid_spec=pltpu.PrefetchScalarGridSpec(
            num_scalar_prefetch=1,
            grid=(1,),
            in_specs=[whole((1, ROWS, TOK))] * 2 + [whole(dy_turned.shape)],
            out_specs=whole(out),
        ),
        out_shape=jax.ShapeDtypeStruct(out, BF16),
        name="projection_term",
        **params(4),
    )(scal, o, o_got, dy_turned)


def shards(queries, keys, values, grad_out, out_proj):
    me = lax.axis_index("ctx")
    blocks = lax.axis_size("ctx")
    odd = me % 2
    below = (me >= 2).astype(jnp.int32)
    above = (me < blocks - 2).astype(jnp.int32)
    scal = jnp.stack(
        [jnp.where(odd == 0, below, above), jnp.where(odd == 0, above, below), odd]
    ).astype(jnp.int32)
    swap_pairs = [(i, i ^ 1) for i in range(blocks)]
    step_a = [(i, i + (2 if i % 2 == 0 else -2)) for i in range(blocks)]
    step_b = [(i, i - (2 if i % 2 == 0 else -2)) for i in range(blocks)]
    step_a = [(i, t) for i, t in step_a if 0 <= t < blocks]
    step_b = [(i, t) for i, t in step_b if 0 <= t < blocks]

    def swap(x):
        return lax.ppermute(x, "ctx", swap_pairs)

    def to_a(x):
        return lax.ppermute(x, "ctx", step_a)

    def to_b(x):
        return lax.ppermute(x, "ctx", step_b)

    dy = grad_out[0]
    kv_mine, kv_send, q_mine, q_send = split_heads(scal, keys[0], values[0], queries[0])
    kv_got = swap(kv_send)
    a_mine, b_mine = to_a(kv_mine), to_b(kv_mine)
    q_got = swap(q_send)
    g_mine, g_send, dy_turned = attention_grad(scal, dy, out_proj)
    g_got = swap(g_send)
    a_got, b_got = to_a(kv_got), to_b(kv_got)
    kv = (a_mine, a_got, kv_mine, kv_got, b_mine, b_got)
    q = (q_mine, q_got)
    g = (g_mine, g_got)
    early_m, early_p, stats = forward((2, 3, 4, 0), scal, q, kv, None, False, 16)
    o_mine, o_send, lse = forward((1, 5), scal, q, kv, (stats, early_m, early_p), True, 8)
    o_got = swap(o_send)
    o = (o_mine, o_send)

    pair = head_major(2)
    work = (scal, q, g, o, lse, kv)
    pa, pb, dq_m, dq_p = backward(0, ((1, 0), (1, 1), (5, 1)), *work, (pair, pair))
    arrived = (to_b(pa), to_a(pb))
    whole_pair = head_major(2, F32)
    outs = (head_major(3), pair, pair, whole_pair)
    pairs = ((3, 0), (3, 1), (0, 0), (4, 0), (4, 1), (2, 1))
    for_partner, pa, pb, mid, dq_m = backward(
        1, pairs, *work, outs, (dq_m, dq_p, *arrived), 24
    )
    got = swap(for_partner)
    back_a, back_b = to_b(pa), to_a(pb)
    rest, dq = backward(2, ((2, 0),), *work, (whole_pair,), (dq_m,), 7)

    dps = lax.axis_size("dp")
    norm = float(TOK * blocks * dps) ** (-0.5)
    term = project(scal, o_mine, o_got, dy_turned, norm)
    term = lax.all_to_all(term.reshape(dps, -1, term.shape[1]), "dp", 0, 0)
    term = jnp.sum(term.astype(F32), axis=0)
    term = term.reshape(blocks, -1, term.shape[1])
    term = lax.all_to_all(term, "ctx", 0, 0)
    proj = jnp.sum(term, axis=0)

    gq, gk, gv = finish(scal, dq, mid, rest, back_a, back_b, got)
    return gq[None], gk[None], gv[None], proj


def solution(mesh):
    rows = P("dp", "ctx", None)
    return jax.shard_map(
        shards,
        mesh=mesh,
        in_specs=(rows, rows, rows, rows, P()),
        out_specs=(rows, rows, rows, P(("dp", "ctx"), None)),
        check_vma=False,
    )
```

```python
import functools
import math

import jax
import jax.numpy as jnp
from jax import lax
from jax.experimental import pallas as pl
from jax.experimental.pallas import tpu as pltpu
from jax.sharding import PartitionSpec as P

HEADS = 10
HDIM = 64
HALF = HEADS // 2
ROWS = HALF * HDIM
TOK = 512
SCALE = HDIM ** (-0.5)
BASE2 = SCALE * math.log2(math.e)
BIG = 1e30
FAR = 48.0
F32 = jnp.float32
BF16 = jnp.bfloat16

UNSEEN = ((5,), (0,))


def params(us):
    return dict(
        compiler_params=pltpu.CompilerParams(vmem_limit_bytes=2**26 - 2**17),
        cost_estimate=pl.CostEstimate(
            flops=int(us * 1.15e9), bytes_accessed=int(us * 1e5), transcendentals=0
        ),
    )


def mm(a, b, ca, cb):
    return lax.dot_general(a, b, (((ca,), (cb,)), ((), ())), preferred_element_type=F32)


def head_block(parts):
    return pl.BlockSpec((parts, HDIM, TOK), lambda h, s: (0, h, 0))


def head_major(parts, dtype=BF16):
    return jax.ShapeDtypeStruct((parts, ROWS, TOK), dtype)


def whole(shape):
    return pl.BlockSpec(shape, lambda i, s: (0,) * len(shape))


def halves(x):
    return x[:ROWS], x[ROWS:]


def in_order(odd, mine, partners):
    first = jnp.where(odd, partners, mine)
    return jnp.concatenate([first, jnp.where(odd, mine, partners)], axis=0)


def split_kernel(scal, k_ref, v_ref, q_ref, kv_mine, kv_send, q_mine, q_send):
    odd = scal[2] > 0
    for n, ref in enumerate((k_ref, v_ref)):
        low, high = halves(jnp.transpose(ref[...]))
        kv_mine[n] = jnp.where(odd, high, low)
        kv_send[n] = jnp.where(odd, low, high)
    low, high = halves(jnp.transpose(q_ref[...]))
    q_mine[0] = jnp.where(odd, high, low)
    q_send[0] = jnp.where(odd, low, high)


def split_heads(scal, k, v, q):
    return pl.pallas_call(
        split_kernel,
        grid_spec=pltpu.PrefetchScalarGridSpec(
            num_scalar_prefetch=1,
            grid=(1,),
            in_specs=[whole(k.shape)] * 3,
            out_specs=[whole((2, ROWS, TOK))] * 2 + [whole((1, ROWS, TOK))] * 2,
        ),
        out_shape=[head_major(2)] * 2 + [head_major(1)] * 2,
        name="split_kvq",
        **params(4),
    )(scal, k, v, q)


def grad_kernel(scal, dy_ref, w_ref, mine, send, dy_turned):
    odd = scal[2] > 0
    low, high = halves(mm(w_ref[...], dy_ref[...], 1, 1).astype(BF16))
    mine[0] = jnp.where(odd, high, low)
    send[0] = jnp.where(odd, low, high)
    dy_turned[...] = jnp.transpose(dy_ref[...])


def attention_grad(scal, dy, w):
    return pl.pallas_call(
        grad_kernel,
        grid_spec=pltpu.PrefetchScalarGridSpec(
            num_scalar_prefetch=1,
            grid=(1,),
            in_specs=[whole(dy.shape), whole(w.shape)],
            out_specs=[whole((1, ROWS, TOK))] * 2 + [whole(dy.shape[::-1])],
        ),
        out_shape=[head_major(1)] * 2 + [jax.ShapeDtypeStruct(dy.shape[::-1], BF16)],
        name="attention_grad",
        **params(4),
    )(scal, dy, w)


def side_flag(scal, j):
    return None if j in (2, 3) else scal[0] if j < 2 else scal[1]


def forward_kernel(js, carry, last, scal, qm, qp, *refs):
    kv, refs = refs[: len(js)], refs[len(js) :]
    qs = (qm[0], qp[0])
    units = [(n, i) for n, j in enumerate(js) for i in (0, 1) if j not in UNSEEN[i]]
    turned = {}

    def scores(n, i):
        if n not in turned:
            turned[n] = jnp.transpose(kv[n][0])
        return mm(turned[n], qs[i], 1, 0)

    if carry:
        stats, o_in, refs = refs[0], refs[1:3], refs[3:]
    om, op, stats_out = refs

    def run(running):
        top, total, out = [None, None], [None, None], [None, None]
        over = None
        if carry:
            for i in (0, 1):
                top[i] = stats[0, i : i + 1, :]
                total[i] = stats[0, 2 + i : 3 + i, :]
                out[i] = o_in[i][0]
        ahead = scores(*units[0])
        for n, (b, i) in enumerate(units):
            s = ahead
            if n + 1 < len(units):
                ahead = scores(*units[n + 1])
            flag = side_flag(scal, js[b])
            here = jnp.max(s, axis=0, keepdims=True) * BASE2
            if flag is not None:
                here = jnp.where(flag > 0, here, -BIG)
            first = top[i] is None
            if first:
                new = here
            elif running:
                new = jnp.maximum(top[i], here)
            else:
                new = top[i]
                over = here - new if over is None else jnp.maximum(over, here - new)
            sub = new if flag is None else jnp.where(flag > 0, new, BIG)
            e = jnp.exp2(s * BASE2 - sub)
            part = jnp.sum(e, axis=0, keepdims=True)
            pv = mm(kv[b][1], e.astype(BF16), 1, 0)
            if first:
                total[i], out[i] = part, pv
            elif running:
                fade = jnp.exp2(top[i] - new)
                total[i] = total[i] * fade + part
                out[i] = out[i] * fade + pv
            else:
                total[i] = total[i] + part
                out[i] = out[i] + pv
            top[i] = new
        for i, ref in ((0, om), (1, op)):
            if last:
                ref[0] = (out[i] * (1.0 / total[i])).astype(BF16)
                stats_out[0, i : i + 1, :] = top[i] + jnp.log2(total[i])
            else:
                ref[0] = out[i]
                stats_out[0, i : i + 1, :] = top[i]
                stats_out[0, 2 + i : 3 + i, :] = total[i]
        return over

    far = jnp.max(run(False)) > FAR

    @pl.when(far)
    def _():
        turned.clear()
        run(True)


def stat_block(rows):
    return pl.BlockSpec((1, rows, TOK), lambda h, s: (h, 0, 0))


def forward(js, scal, q, kv, carry, last, us):
    given = () if carry is None else carry
    rows = 2 if last else 4
    return pl.pallas_call(
        functools.partial(forward_kernel, js, bool(given), last),
        grid_spec=pltpu.PrefetchScalarGridSpec(
            num_scalar_prefetch=1,
            grid=(HALF,),
            in_specs=[head_block(1)] * 2
            + [head_block(2)] * len(js)
            + ([stat_block(4)] + [head_block(1)] * 2 if given else []),
            out_specs=[head_block(1)] * 2 + [stat_block(rows)],
        ),
        out_shape=[head_major(1, BF16 if last else F32)] * 2
        + [jax.ShapeDtypeStruct((HALF, rows, TOK), F32)],
        name="forward_" + "".join(str(j) for j in js),
        **params(us),
    )(scal, *q, *[kv[j] for j in js], *given)


def backward_kernel(js, pairs, stage, scal, qm, qp, gm, gp, om, op, lse, *refs):
    n = len(js)
    kv, refs = refs[:n], refs[n:]
    mine, partners = any(i == 0 for _, i in pairs), any(i == 1 for _, i in pairs)
    dq_in = ()
    if stage > 0:
        dq_in, refs = refs[: mine + partners], refs[mine + partners :]
    if stage == 1:
        arrived, refs = refs[:2], refs[2:]
    dkv, dq_out = refs[:n], refs[n:]
    qs = (qm[0], qp[0])
    gs = (gm[0], gp[0])
    os = (om[0], op[0])
    ls = [lse[0, i : i + 1, :] for i in (0, 1)]
    delta = [
        jnp.sum(gs[i].astype(F32) * os[i].astype(F32), axis=0, keepdims=True) for i in (0, 1)
    ]
    q_turned = [jnp.transpose(x) for x in qs]
    dq = [x[0] for x in dq_in] if stage > 0 else [None, None]
    units = [(js.index(j), i) for j, i in pairs]
    turned = {}

    def products(idx, i):
        if idx not in turned:
            turned[idx] = (jnp.transpose(kv[idx][0]), jnp.transpose(kv[idx][1]))
        k, v = turned[idx]
        return mm(k, qs[i], 1, 0), mm(v, gs[i], 1, 0)

    ahead = products(*units[0])
    dk = dv = None
    for n, (idx, i) in enumerate(units):
        s, dp = ahead
        if n + 1 < len(units):
            ahead = products(*units[n + 1])
        flag = side_flag(scal, js[idx])
        sub = ls[i] if flag is None else jnp.where(flag > 0, ls[i], BIG)
        p = jnp.exp2(s * BASE2 - sub)
        ds = (p * (dp - delta[i])).astype(BF16)
        a = mm(gs[i], p.astype(BF16), 1, 1)
        b = mm(ds, q_turned[i], 1, 0)
        dv = a if dv is None else dv + a
        dk = b if dk is None else dk + b
        x = mm(kv[idx][0], ds, 1, 0)
        dq[i] = x if dq[i] is None else dq[i] + x
        if n + 1 == len(units) or units[n + 1][0] != idx:
            dk = jnp.transpose(dk) * SCALE
            if stage == 1 and js[idx] == 3:
                dk = dk + arrived[0][0].astype(F32) + arrived[1][0].astype(F32)
                dv = dv + arrived[0][1].astype(F32) + arrived[1][1].astype(F32)
            dkv[idx][0] = dk.astype(dkv[idx].dtype)
            dkv[idx][1] = dv.astype(dkv[idx].dtype)
            dk = dv = None
    if stage == 0:
        dq_out[0][0] = dq[0]
        dq_out[1][0] = dq[1]
    elif stage == 1:
        dkv[js.index(3)][2] = (dq[1] * SCALE).astype(BF16)
        dq_out[0][0] = dq[0]
    else:
        dq_out[0][0] = (dq[0] * SCALE).astype(BF16)


def backward(stage, pairs, scal, q, g, o, lse, kv, outs, given=(), us=13):
    js = tuple(dict.fromkeys(j for j, _ in pairs))
    dq_out = [head_major(1, BF16 if stage == 2 else F32)] * (2 if stage == 0 else 1)
    return pl.pallas_call(
        functools.partial(backward_kernel, js, pairs, stage),
        grid_spec=pltpu.PrefetchScalarGridSpec(
            num_scalar_prefetch=1,
            grid=(HALF,),
            in_specs=[head_block(1)] * 6
            + [stat_block(2)]
            + [head_block(2)] * len(js)
            + [head_block(x.shape[0]) for x in given],
            out_specs=[head_block(x.shape[0]) for x in outs]
            + [head_block(1)] * len(dq_out),
        ),
        out_shape=list(outs) + dq_out,
        name="backward_" + "".join(str(j) for j in js),
        **params(us),
    )(scal, *q, *g, *o, lse, *[kv[j] for j in js], *given)


def finish_kernel(scal, dq, mid, rest, a, b, got, gq, gk, gv):
    odd = scal[2] > 0
    gq[...] = jnp.transpose(in_order(odd, dq[0], got[2]))
    for n, ref in ((0, gk), (1, gv)):
        total = mid[n] + rest[n] + a[n].astype(F32) + b[n].astype(F32)
        ref[...] = jnp.transpose(in_order(odd, total.astype(BF16), got[n]))


def finish(scal, dq, mid, rest, a, b, got):
    out = (TOK, 2 * ROWS)
    return pl.pallas_call(
        finish_kernel,
        grid_spec=pltpu.PrefetchScalarGridSpec(
            num_scalar_prefetch=1,
            grid=(1,),
            in_specs=[whole((1, ROWS, TOK))]
            + [whole((2, ROWS, TOK))] * 4
            + [whole((3, ROWS, TOK))],
            out_specs=[whole(out)] * 3,
        ),
        out_shape=[jax.ShapeDtypeStruct(out, BF16)] * 3,
        name="sum_and_turn",
        **params(4),
    )(scal, dq, mid, rest, a, b, got)


def project_kernel(norm, scal, o, o_got, dy_turned, term):
    attn = in_order(scal[2] > 0, o[0], o_got[0])
    term[...] = (mm(dy_turned[...], attn, 1, 1) * norm).astype(BF16)


def project(scal, o, o_got, dy_turned, norm):
    out = (dy_turned.shape[0], 2 * ROWS)
    return pl.pallas_call(
        functools.partial(project_kernel, norm),
        grid_spec=pltpu.PrefetchScalarGridSpec(
            num_scalar_prefetch=1,
            grid=(1,),
            in_specs=[whole((1, ROWS, TOK))] * 2 + [whole(dy_turned.shape)],
            out_specs=whole(out),
        ),
        out_shape=jax.ShapeDtypeStruct(out, BF16),
        name="projection_term",
        **params(4),
    )(scal, o, o_got, dy_turned)


def shards(queries, keys, values, grad_out, out_proj):
    me = lax.axis_index("ctx")
    blocks = lax.axis_size("ctx")
    odd = me % 2
    below = (me >= 2).astype(jnp.int32)
    above = (me < blocks - 2).astype(jnp.int32)
    scal = jnp.stack(
        [jnp.where(odd == 0, below, above), jnp.where(odd == 0, above, below), odd]
    ).astype(jnp.int32)
    swap_pairs = [(i, i ^ 1) for i in range(blocks)]
    step_a = [(i, i + (2 if i % 2 == 0 else -2)) for i in range(blocks)]
    step_b = [(i, i - (2 if i % 2 == 0 else -2)) for i in range(blocks)]
    step_a = [(i, t) for i, t in step_a if 0 <= t < blocks]
    step_b = [(i, t) for i, t in step_b if 0 <= t < blocks]

    def swap(x):
        return lax.ppermute(x, "ctx", swap_pairs)

    def to_a(x):
        return lax.ppermute(x, "ctx", step_a)

    def to_b(x):
        return lax.ppermute(x, "ctx", step_b)

    dy = grad_out[0]
    kv_mine, kv_send, q_mine, q_send = split_heads(scal, keys[0], values[0], queries[0])
    kv_got = swap(kv_send)
    a_mine, b_mine = to_a(kv_mine), to_b(kv_mine)
    q_got = swap(q_send)
    g_mine, g_send, dy_turned = attention_grad(scal, dy, out_proj)
    g_send, q_got = lax.optimization_barrier((g_send, q_got))
    g_got = swap(g_send)
    a_got, b_got = to_a(kv_got), to_b(kv_got)
    kv = (a_mine, a_got, kv_mine, kv_got, b_mine, b_got)
    q = (q_mine, q_got)
    g = (g_mine, g_got)
    early_m, early_p, stats = forward((2, 3, 4, 0), scal, q, kv, None, False, 16)
    o_mine, o_send, lse = forward((1, 5), scal, q, kv, (stats, early_m, early_p), True, 8)
    o_got = swap(o_send)
    o = (o_mine, o_send)

    pair = head_major(2)
    work = (scal, q, g, o, lse, kv)
    pa, pb, dq_m, dq_p = backward(0, ((1, 0), (1, 1), (5, 1)), *work, (pair, pair))
    arrived = (to_b(pa), to_a(pb))
    whole_pair = head_major(2, F32)
    outs = (head_major(3), pair, pair, whole_pair)
    pairs = ((3, 0), (3, 1), (0, 0), (4, 0), (4, 1), (2, 1))
    for_partner, pa, pb, mid, dq_m = backward(
        1, pairs, *work, outs, (dq_m, dq_p, *arrived), 24
    )
    got = swap(for_partner)
    back_a, back_b = to_b(pa), to_a(pb)
    rest, dq = backward(2, ((2, 0),), *work, (whole_pair,), (dq_m,), 7)

    dps = lax.axis_size("dp")
    norm = float(TOK * blocks * dps) ** (-0.5)
    term = project(scal, o_mine, o_got, dy_turned, norm)
    term = lax.all_to_all(term.reshape(dps, -1, term.shape[1]), "dp", 0, 0)
    term = jnp.sum(term.astype(F32), axis=0)
    term = term.reshape(blocks, -1, term.shape[1])
    term = lax.all_to_all(term, "ctx", 0, 0)
    proj = jnp.sum(term, axis=0)

    proj, dq = lax.optimization_barrier((proj, dq))
    gq, gk, gv = finish(scal, dq, mid, rest, back_a, back_b, got)
    return gq[None], gk[None], gv[None], proj


def solution(mesh):
    rows = P("dp", "ctx", None)
    return jax.shard_map(
        shards,
        mesh=mesh,
        in_specs=(rows, rows, rows, rows, P()),
        out_specs=(rows, rows, rows, P(("dp", "ctx"), None)),
        check_vma=False,
    )
```

```python
import functools
import math

import jax
import jax.numpy as jnp
from jax import lax
from jax.experimental import pallas as pl
from jax.experimental.pallas import tpu as pltpu
from jax.sharding import PartitionSpec as P

HEADS = 10
HDIM = 64
HALF = HEADS // 2
ROWS = HALF * HDIM
TOK = 512
SCALE = HDIM ** (-0.5)
BASE2 = SCALE * math.log2(math.e)
BIG = 1e30
FAR = 48.0
F32 = jnp.float32
BF16 = jnp.bfloat16

UNSEEN = ((5,), (0,))


def params(us):
    return dict(
        compiler_params=pltpu.CompilerParams(vmem_limit_bytes=2**26 - 2**17),
        cost_estimate=pl.CostEstimate(
            flops=int(us * 1.15e9), bytes_accessed=int(us * 1e5), transcendentals=0
        ),
    )


def mm(a, b, ca, cb):
    return lax.dot_general(a, b, (((ca,), (cb,)), ((), ())), preferred_element_type=F32)


def head_block(parts):
    return pl.BlockSpec((parts, HDIM, TOK), lambda h, s: (0, h, 0))


def head_major(parts, dtype=BF16):
    return jax.ShapeDtypeStruct((parts, ROWS, TOK), dtype)


def whole(shape):
    return pl.BlockSpec(shape, lambda i, s: (0,) * len(shape))


def halves(x):
    return x[:ROWS], x[ROWS:]


def in_order(odd, mine, partners):
    first = jnp.where(odd, partners, mine)
    return jnp.concatenate([first, jnp.where(odd, mine, partners)], axis=0)


def split_kernel(scal, k_ref, v_ref, q_ref, kv_mine, kv_send, q_mine, q_send):
    odd = scal[2] > 0
    for n, ref in enumerate((k_ref, v_ref)):
        low, high = halves(jnp.transpose(ref[...]))
        kv_mine[n] = jnp.where(odd, high, low)
        kv_send[n] = jnp.where(odd, low, high)
    low, high = halves(jnp.transpose(q_ref[...]))
    q_mine[0] = jnp.where(odd, high, low)
    q_send[0] = jnp.where(odd, low, high)


def split_heads(scal, k, v, q):
    return pl.pallas_call(
        split_kernel,
        grid_spec=pltpu.PrefetchScalarGridSpec(
            num_scalar_prefetch=1,
            grid=(1,),
            in_specs=[whole(k.shape)] * 3,
            out_specs=[whole((2, ROWS, TOK))] * 2 + [whole((1, ROWS, TOK))] * 2,
        ),
        out_shape=[head_major(2)] * 2 + [head_major(1)] * 2,
        name="split_kvq",
        **params(4),
    )(scal, k, v, q)


def grad_kernel(scal, dy_ref, w_ref, mine, send, dy_turned):
    odd = scal[2] > 0
    low, high = halves(mm(w_ref[...], dy_ref[...], 1, 1).astype(BF16))
    mine[0] = jnp.where(odd, high, low)
    send[0] = jnp.where(odd, low, high)
    dy_turned[...] = jnp.transpose(dy_ref[...])


def attention_grad(scal, dy, w):
    return pl.pallas_call(
        grad_kernel,
        grid_spec=pltpu.PrefetchScalarGridSpec(
            num_scalar_prefetch=1,
            grid=(1,),
            in_specs=[whole(dy.shape), whole(w.shape)],
            out_specs=[whole((1, ROWS, TOK))] * 2 + [whole(dy.shape[::-1])],
        ),
        out_shape=[head_major(1)] * 2 + [jax.ShapeDtypeStruct(dy.shape[::-1], BF16)],
        name="attention_grad",
        **params(4),
    )(scal, dy, w)


def side_flag(scal, j):
    return None if j in (2, 3) else scal[0] if j < 2 else scal[1]


def forward_kernel(js, carry, last, scal, qm, qp, *refs):
    kv, refs = refs[: len(js)], refs[len(js) :]
    qs = (qm[0], qp[0])
    units = [(n, i) for n, j in enumerate(js) for i in (0, 1) if j not in UNSEEN[i]]
    turned = {}

    def scores(n, i):
        if n not in turned:
            turned[n] = jnp.transpose(kv[n][0])
        return mm(turned[n], qs[i], 1, 0)

    if carry:
        stats, o_in, refs = refs[0], refs[1:3], refs[3:]
    om, op, stats_out = refs

    def run(running):
        top, total, out = [None, None], [None, None], [None, None]
        over = None
        if carry:
            for i in (0, 1):
                top[i] = stats[0, i : i + 1, :]
                total[i] = stats[0, 2 + i : 3 + i, :]
                out[i] = o_in[i][0]
        ahead = scores(*units[0])
        for n, (b, i) in enumerate(units):
            s = ahead
            if n + 1 < len(units):
                ahead = scores(*units[n + 1])
            flag = side_flag(scal, js[b])
            here = jnp.max(s, axis=0, keepdims=True) * BASE2
            if flag is not None:
                here = jnp.where(flag > 0, here, -BIG)
            first = top[i] is None
            if first:
                new = here
            elif running:
                new = jnp.maximum(top[i], here)
            else:
                new = top[i]
                over = here - new if over is None else jnp.maximum(over, here - new)
            sub = new if flag is None else jnp.where(flag > 0, new, BIG)
            e = jnp.exp2(s * BASE2 - sub)
            part = jnp.sum(e, axis=0, keepdims=True)
            pv = mm(kv[b][1], e.astype(BF16), 1, 0)
            if first:
                total[i], out[i] = part, pv
            elif running:
                fade = jnp.exp2(top[i] - new)
                total[i] = total[i] * fade + part
                out[i] = out[i] * fade + pv
            else:
                total[i] = total[i] + part
                out[i] = out[i] + pv
            top[i] = new
        for i, ref in ((0, om), (1, op)):
            if last:
                ref[0] = (out[i] * (1.0 / total[i])).astype(BF16)
                stats_out[0, i : i + 1, :] = top[i] + jnp.log2(total[i])
            else:
                ref[0] = out[i]
                stats_out[0, i : i + 1, :] = top[i]
                stats_out[0, 2 + i : 3 + i, :] = total[i]
        return over

    far = jnp.max(run(False)) > FAR

    @pl.when(far)
    def _():
        turned.clear()
        run(True)


def stat_block(rows):
    return pl.BlockSpec((1, rows, TOK), lambda h, s: (h, 0, 0))


def forward(js, scal, q, kv, carry, last, us):
    given = () if carry is None else carry
    rows = 2 if last else 4
    return pl.pallas_call(
        functools.partial(forward_kernel, js, bool(given), last),
        grid_spec=pltpu.PrefetchScalarGridSpec(
            num_scalar_prefetch=1,
            grid=(HALF,),
            in_specs=[head_block(1)] * 2
            + [head_block(2)] * len(js)
            + ([stat_block(4)] + [head_block(1)] * 2 if given else []),
            out_specs=[head_block(1)] * 2 + [stat_block(rows)],
        ),
        out_shape=[head_major(1, BF16 if last else F32)] * 2
        + [jax.ShapeDtypeStruct((HALF, rows, TOK), F32)],
        name="forward_" + "".join(str(j) for j in js),
        **params(us),
    )(scal, *q, *[kv[j] for j in js], *given)


def backward_kernel(js, pairs, stage, scal, qm, qp, gm, gp, om, op, lse, *refs):
    n = len(js)
    kv, refs = refs[:n], refs[n:]
    mine, partners = any(i == 0 for _, i in pairs), any(i == 1 for _, i in pairs)
    dq_in = ()
    if stage > 0:
        dq_in, refs = refs[: mine + partners], refs[mine + partners :]
    if stage == 1:
        arrived, refs = refs[:2], refs[2:]
    dkv, dq_out = refs[:n], refs[n:]
    qs = (qm[0], qp[0])
    gs = (gm[0], gp[0])
    os = (om[0], op[0])
    ls = [lse[0, i : i + 1, :] for i in (0, 1)]
    delta = [
        jnp.sum(gs[i].astype(F32) * os[i].astype(F32), axis=0, keepdims=True) for i in (0, 1)
    ]
    q_turned = [jnp.transpose(x) for x in qs]
    dq = [x[0] for x in dq_in] if stage > 0 else [None, None]
    units = [(js.index(j), i) for j, i in pairs]
    turned = {}

    def products(idx, i):
        if idx not in turned:
            turned[idx] = (jnp.transpose(kv[idx][0]), jnp.transpose(kv[idx][1]))
        k, v = turned[idx]
        return mm(k, qs[i], 1, 0), mm(v, gs[i], 1, 0)

    ahead = products(*units[0])
    dk = dv = None
    for n, (idx, i) in enumerate(units):
        s, dp = ahead
        if n + 1 < len(units):
            ahead = products(*units[n + 1])
        flag = side_flag(scal, js[idx])
        sub = ls[i] if flag is None else jnp.where(flag > 0, ls[i], BIG)
        p = jnp.exp2(s * BASE2 - sub)
        ds = (p * (dp - delta[i])).astype(BF16)
        a = mm(gs[i], p.astype(BF16), 1, 1)
        b = mm(ds, q_turned[i], 1, 0)
        dv = a if dv is None else dv + a
        dk = b if dk is None else dk + b
        x = mm(kv[idx][0], ds, 1, 0)
        dq[i] = x if dq[i] is None else dq[i] + x
        if n + 1 == len(units) or units[n + 1][0] != idx:
            dk = jnp.transpose(dk) * SCALE
            if stage == 1 and js[idx] == 3:
                dk = dk + arrived[0][0].astype(F32) + arrived[1][0].astype(F32)
                dv = dv + arrived[0][1].astype(F32) + arrived[1][1].astype(F32)
            dkv[idx][0] = dk.astype(dkv[idx].dtype)
            dkv[idx][1] = dv.astype(dkv[idx].dtype)
            dk = dv = None
    if stage == 0:
        dq_out[0][0] = dq[0]
        dq_out[1][0] = dq[1]
    elif stage == 1:
        dkv[js.index(3)][2] = (dq[1] * SCALE).astype(BF16)
        dq_out[0][0] = dq[0]
    else:
        dq_out[0][0] = (dq[0] * SCALE).astype(BF16)


def backward(stage, pairs, scal, q, g, o, lse, kv, outs, given=(), us=13):
    js = tuple(dict.fromkeys(j for j, _ in pairs))
    dq_out = [head_major(1, BF16 if stage == 2 else F32)] * (2 if stage == 0 else 1)
    return pl.pallas_call(
        functools.partial(backward_kernel, js, pairs, stage),
        grid_spec=pltpu.PrefetchScalarGridSpec(
            num_scalar_prefetch=1,
            grid=(HALF,),
            in_specs=[head_block(1)] * 6
            + [stat_block(2)]
            + [head_block(2)] * len(js)
            + [head_block(x.shape[0]) for x in given],
            out_specs=[head_block(x.shape[0]) for x in outs]
            + [head_block(1)] * len(dq_out),
        ),
        out_shape=list(outs) + dq_out,
        name="backward_" + "".join(str(j) for j in js),
        **params(us),
    )(scal, *q, *g, *o, lse, *[kv[j] for j in js], *given)


def finish_kernel(scal, dq, mid, rest, a, b, got, gq, gk, gv):
    odd = scal[2] > 0
    gq[...] = jnp.transpose(in_order(odd, dq[0], got[2]))
    for n, ref in ((0, gk), (1, gv)):
        total = mid[n] + rest[n] + a[n].astype(F32) + b[n].astype(F32)
        ref[...] = jnp.transpose(in_order(odd, total.astype(BF16), got[n]))


def finish(scal, dq, mid, rest, a, b, got):
    out = (TOK, 2 * ROWS)
    return pl.pallas_call(
        finish_kernel,
        grid_spec=pltpu.PrefetchScalarGridSpec(
            num_scalar_prefetch=1,
            grid=(1,),
            in_specs=[whole((1, ROWS, TOK))]
            + [whole((2, ROWS, TOK))] * 4
            + [whole((3, ROWS, TOK))],
            out_specs=[whole(out)] * 3,
        ),
        out_shape=[jax.ShapeDtypeStruct(out, BF16)] * 3,
        name="sum_and_turn",
        **params(0.1),
    )(scal, dq, mid, rest, a, b, got)


def project_kernel(norm, scal, o, o_got, dy_turned, term):
    attn = in_order(scal[2] > 0, o[0], o_got[0])
    term[...] = (mm(dy_turned[...], attn, 1, 1) * norm).astype(BF16)


def project(scal, o, o_got, dy_turned, norm):
    out = (dy_turned.shape[0], 2 * ROWS)
    return pl.pallas_call(
        functools.partial(project_kernel, norm),
        grid_spec=pltpu.PrefetchScalarGridSpec(
            num_scalar_prefetch=1,
            grid=(1,),
            in_specs=[whole((1, ROWS, TOK))] * 2 + [whole(dy_turned.shape)],
            out_specs=whole(out),
        ),
        out_shape=jax.ShapeDtypeStruct(out, BF16),
        name="projection_term",
        **params(4),
    )(scal, o, o_got, dy_turned)


def shards(queries, keys, values, grad_out, out_proj):
    me = lax.axis_index("ctx")
    blocks = lax.axis_size("ctx")
    odd = me % 2
    below = (me >= 2).astype(jnp.int32)
    above = (me < blocks - 2).astype(jnp.int32)
    scal = jnp.stack(
        [jnp.where(odd == 0, below, above), jnp.where(odd == 0, above, below), odd]
    ).astype(jnp.int32)
    swap_pairs = [(i, i ^ 1) for i in range(blocks)]
    step_a = [(i, i + (2 if i % 2 == 0 else -2)) for i in range(blocks)]
    step_b = [(i, i - (2 if i % 2 == 0 else -2)) for i in range(blocks)]
    step_a = [(i, t) for i, t in step_a if 0 <= t < blocks]
    step_b = [(i, t) for i, t in step_b if 0 <= t < blocks]

    def swap(x):
        return lax.ppermute(x, "ctx", swap_pairs)

    def to_a(x):
        return lax.ppermute(x, "ctx", step_a)

    def to_b(x):
        return lax.ppermute(x, "ctx", step_b)

    dy = grad_out[0]
    kv_mine, kv_send, q_mine, q_send = split_heads(scal, keys[0], values[0], queries[0])
    kv_got = swap(kv_send)
    a_mine, b_mine = to_a(kv_mine), to_b(kv_mine)
    q_got = swap(q_send)
    g_mine, g_send, dy_turned = attention_grad(scal, dy, out_proj)
    g_got = swap(g_send)
    a_got, b_got = to_a(kv_got), to_b(kv_got)
    kv = (a_mine, a_got, kv_mine, kv_got, b_mine, b_got)
    q = (q_mine, q_got)
    g = (g_mine, g_got)
    early_m, early_p, stats = forward((2, 3, 4, 0), scal, q, kv, None, False, 16)
    o_mine, o_send, lse = forward((1, 5), scal, q, kv, (stats, early_m, early_p), True, 8)
    o_got = swap(o_send)
    o = (o_mine, o_send)

    pair = head_major(2)
    work = (scal, q, g, o, lse, kv)
    pa, pb, dq_m, dq_p = backward(0, ((1, 0), (1, 1), (5, 1)), *work, (pair, pair))
    arrived = (to_b(pa), to_a(pb))
    whole_pair = head_major(2, F32)
    outs = (head_major(3), pair, pair, whole_pair)
    pairs = ((3, 0), (3, 1), (0, 0), (4, 0), (4, 1), (2, 1))
    for_partner, pa, pb, mid, dq_m = backward(
        1, pairs, *work, outs, (dq_m, dq_p, *arrived), 24
    )
    got = swap(for_partner)
    back_a, back_b = to_b(pa), to_a(pb)
    rest, dq = backward(2, ((2, 0),), *work, (whole_pair,), (dq_m,), 7)

    dps = lax.axis_size("dp")
    norm = float(TOK * blocks * dps) ** (-0.5)
    term = project(scal, o_mine, o_got, dy_turned, norm)
    term = lax.all_to_all(term.reshape(dps, -1, term.shape[1]), "dp", 0, 0)
    term = jnp.sum(term.astype(F32), axis=0)
    term = term.reshape(blocks, -1, term.shape[1])
    term = lax.all_to_all(term, "ctx", 0, 0)
    proj = jnp.sum(term, axis=0)

    gq, gk, gv = finish(scal, dq, mid, rest, back_a, back_b, got)
    return gq[None], gk[None], gv[None], proj


def solution(mesh):
    rows = P("dp", "ctx", None)
    return jax.shard_map(
        shards,
        mesh=mesh,
        in_specs=(rows, rows, rows, rows, P()),
        out_specs=(rows, rows, rows, P(("dp", "ctx"), None)),
        check_vma=False,
    )
```

```python
import functools
import math

import jax
import jax.numpy as jnp
from jax import lax
from jax.experimental import pallas as pl
from jax.experimental.pallas import tpu as pltpu
from jax.sharding import PartitionSpec as P

HEADS = 10
HDIM = 64
HALF = HEADS // 2
ROWS = HALF * HDIM
TOK = 512
SCALE = HDIM ** (-0.5)
BASE2 = SCALE * math.log2(math.e)
BIG = 1e30
FAR = 48.0
F32 = jnp.float32
BF16 = jnp.bfloat16

UNSEEN = ((5,), (0,))


def params(us):
    return dict(
        compiler_params=pltpu.CompilerParams(vmem_limit_bytes=2**26 - 2**17),
        cost_estimate=pl.CostEstimate(
            flops=int(us * 1.15e9), bytes_accessed=int(us * 1e5), transcendentals=0
        ),
    )


def mm(a, b, ca, cb):
    return lax.dot_general(a, b, (((ca,), (cb,)), ((), ())), preferred_element_type=F32)


def head_block(parts):
    return pl.BlockSpec((parts, HDIM, TOK), lambda h, s: (0, h, 0))


def head_major(parts, dtype=BF16):
    return jax.ShapeDtypeStruct((parts, ROWS, TOK), dtype)


def whole(shape):
    return pl.BlockSpec(shape, lambda i, s: (0,) * len(shape))


def halves(x):
    return x[:ROWS], x[ROWS:]


def in_order(odd, mine, partners):
    first = jnp.where(odd, partners, mine)
    return jnp.concatenate([first, jnp.where(odd, mine, partners)], axis=0)


def split_kernel(scal, *refs):
    odd = scal[2] > 0
    *sources, mine, send = refs
    for n, ref in enumerate(sources):
        low, high = halves(jnp.transpose(ref[...]))
        mine[n] = jnp.where(odd, high, low)
        send[n] = jnp.where(odd, low, high)


def split_heads(scal, name, *sources):
    n = len(sources)
    return pl.pallas_call(
        split_kernel,
        grid_spec=pltpu.PrefetchScalarGridSpec(
            num_scalar_prefetch=1,
            grid=(1,),
            in_specs=[whole(sources[0].shape)] * n,
            out_specs=[whole((n, ROWS, TOK))] * 2,
        ),
        out_shape=[head_major(n)] * 2,
        name=name,
        **params(1.3 * n),
    )(scal, *sources)


def grad_kernel(scal, dy_ref, w_ref, mine, send, dy_turned):
    odd = scal[2] > 0
    low, high = halves(mm(w_ref[...], dy_ref[...], 1, 1).astype(BF16))
    mine[0] = jnp.where(odd, high, low)
    send[0] = jnp.where(odd, low, high)
    dy_turned[...] = jnp.transpose(dy_ref[...])


def attention_grad(scal, dy, w):
    return pl.pallas_call(
        grad_kernel,
        grid_spec=pltpu.PrefetchScalarGridSpec(
            num_scalar_prefetch=1,
            grid=(1,),
            in_specs=[whole(dy.shape), whole(w.shape)],
            out_specs=[whole((1, ROWS, TOK))] * 2 + [whole(dy.shape[::-1])],
        ),
        out_shape=[head_major(1)] * 2 + [jax.ShapeDtypeStruct(dy.shape[::-1], BF16)],
        name="attention_grad",
        **params(4),
    )(scal, dy, w)


def side_flag(scal, j):
    return None if j in (2, 3) else scal[0] if j < 2 else scal[1]


def forward_kernel(js, carry, last, scal, qm, qp, *refs):
    kv, refs = refs[: len(js)], refs[len(js) :]
    qs = (qm[0], qp[0])
    units = [(n, i) for n, j in enumerate(js) for i in (0, 1) if j not in UNSEEN[i]]
    turned = {}

    def scores(n, i):
        if n not in turned:
            turned[n] = jnp.transpose(kv[n][0])
        return mm(turned[n], qs[i], 1, 0)

    if carry:
        stats, o_in, refs = refs[0], refs[1:3], refs[3:]
    om, op, stats_out = refs

    def run(running):
        top, total, out = [None, None], [None, None], [None, None]
        over = None
        if carry:
            for i in (0, 1):
                top[i] = stats[0, i : i + 1, :]
                total[i] = stats[0, 2 + i : 3 + i, :]
                out[i] = o_in[i][0]
        ahead = scores(*units[0])
        for n, (b, i) in enumerate(units):
            s = ahead
            if n + 1 < len(units):
                ahead = scores(*units[n + 1])
            flag = side_flag(scal, js[b])
            here = jnp.max(s, axis=0, keepdims=True) * BASE2
            if flag is not None:
                here = jnp.where(flag > 0, here, -BIG)
            first = top[i] is None
            if first:
                new = here
            elif running:
                new = jnp.maximum(top[i], here)
            else:
                new = top[i]
                over = here - new if over is None else jnp.maximum(over, here - new)
            sub = new if flag is None else jnp.where(flag > 0, new, BIG)
            e = jnp.exp2(s * BASE2 - sub)
            part = jnp.sum(e, axis=0, keepdims=True)
            pv = mm(kv[b][1], e.astype(BF16), 1, 0)
            if first:
                total[i], out[i] = part, pv
            elif running:
                fade = jnp.exp2(top[i] - new)
                total[i] = total[i] * fade + part
                out[i] = out[i] * fade + pv
            else:
                total[i] = total[i] + part
                out[i] = out[i] + pv
            top[i] = new
        for i, ref in ((0, om), (1, op)):
            if last:
                ref[0] = (out[i] * (1.0 / total[i])).astype(BF16)
                stats_out[0, i : i + 1, :] = top[i] + jnp.log2(total[i])
            else:
                ref[0] = out[i]
                stats_out[0, i : i + 1, :] = top[i]
                stats_out[0, 2 + i : 3 + i, :] = total[i]
        return over

    far = jnp.max(run(False)) > FAR

    @pl.when(far)
    def _():
        turned.clear()
        run(True)


def stat_block(rows):
    return pl.BlockSpec((1, rows, TOK), lambda h, s: (h, 0, 0))


def forward(js, scal, q, kv, carry, last, us):
    given = () if carry is None else carry
    rows = 2 if last else 4
    return pl.pallas_call(
        functools.partial(forward_kernel, js, bool(given), last),
        grid_spec=pltpu.PrefetchScalarGridSpec(
            num_scalar_prefetch=1,
            grid=(HALF,),
            in_specs=[head_block(1)] * 2
            + [head_block(2)] * len(js)
            + ([stat_block(4)] + [head_block(1)] * 2 if given else []),
            out_specs=[head_block(1)] * 2 + [stat_block(rows)],
        ),
        out_shape=[head_major(1, BF16 if last else F32)] * 2
        + [jax.ShapeDtypeStruct((HALF, rows, TOK), F32)],
        name="forward_" + "".join(str(j) for j in js),
        **params(us),
    )(scal, *q, *[kv[j] for j in js], *given)


def backward_kernel(js, pairs, stage, scal, qm, qp, gm, gp, om, op, lse, *refs):
    n = len(js)
    kv, refs = refs[:n], refs[n:]
    mine, partners = any(i == 0 for _, i in pairs), any(i == 1 for _, i in pairs)
    dq_in = ()
    if stage > 0:
        dq_in, refs = refs[: mine + partners], refs[mine + partners :]
    if stage == 1:
        arrived, refs = refs[:2], refs[2:]
    dkv, dq_out = refs[:n], refs[n:]
    qs = (qm[0], qp[0])
    gs = (gm[0], gp[0])
    os = (om[0], op[0])
    ls = [lse[0, i : i + 1, :] for i in (0, 1)]
    delta = [
        jnp.sum(gs[i].astype(F32) * os[i].astype(F32), axis=0, keepdims=True) for i in (0, 1)
    ]
    q_turned = [jnp.transpose(x) for x in qs]
    dq = [x[0] for x in dq_in] if stage > 0 else [None, None]
    units = [(js.index(j), i) for j, i in pairs]
    turned = {}

    def products(idx, i):
        if idx not in turned:
            turned[idx] = (jnp.transpose(kv[idx][0]), jnp.transpose(kv[idx][1]))
        k, v = turned[idx]
        return mm(k, qs[i], 1, 0), mm(v, gs[i], 1, 0)

    ahead = products(*units[0])
    dk = dv = None
    for n, (idx, i) in enumerate(units):
        s, dp = ahead
        if n + 1 < len(units):
            ahead = products(*units[n + 1])
        flag = side_flag(scal, js[idx])
        sub = ls[i] if flag is None else jnp.where(flag > 0, ls[i], BIG)
        p = jnp.exp2(s * BASE2 - sub)
        ds = (p * (dp - delta[i])).astype(BF16)
        a = mm(gs[i], p.astype(BF16), 1, 1)
        b = mm(ds, q_turned[i], 1, 0)
        dv = a if dv is None else dv + a
        dk = b if dk is None else dk + b
        x = mm(kv[idx][0], ds, 1, 0)
        dq[i] = x if dq[i] is None else dq[i] + x
        if n + 1 == len(units) or units[n + 1][0] != idx:
            dk = jnp.transpose(dk) * SCALE
            if stage == 1 and js[idx] == 3:
                dk = dk + arrived[0][0].astype(F32) + arrived[1][0].astype(F32)
                dv = dv + arrived[0][1].astype(F32) + arrived[1][1].astype(F32)
            dkv[idx][0] = dk.astype(dkv[idx].dtype)
            dkv[idx][1] = dv.astype(dkv[idx].dtype)
            dk = dv = None
    if stage == 0:
        dq_out[0][0] = dq[0]
        dq_out[1][0] = dq[1]
    elif stage == 1:
        dkv[js.index(3)][2] = (dq[1] * SCALE).astype(BF16)
        dq_out[0][0] = dq[0]
    else:
        dq_out[0][0] = (dq[0] * SCALE).astype(BF16)


def backward(stage, pairs, scal, q, g, o, lse, kv, outs, given=(), us=13):
    js = tuple(dict.fromkeys(j for j, _ in pairs))
    dq_out = [head_major(1, BF16 if stage == 2 else F32)] * (2 if stage == 0 else 1)
    return pl.pallas_call(
        functools.partial(backward_kernel, js, pairs, stage),
        grid_spec=pltpu.PrefetchScalarGridSpec(
            num_scalar_prefetch=1,
            grid=(HALF,),
            in_specs=[head_block(1)] * 6
            + [stat_block(2)]
            + [head_block(2)] * len(js)
            + [head_block(x.shape[0]) for x in given],
            out_specs=[head_block(x.shape[0]) for x in outs]
            + [head_block(1)] * len(dq_out),
        ),
        out_shape=list(outs) + dq_out,
        name="backward_" + "".join(str(j) for j in js),
        **params(us),
    )(scal, *q, *g, *o, lse, *[kv[j] for j in js], *given)


def finish_kernel(scal, dq, mid, rest, a, b, got, gq, gk, gv):
    odd = scal[2] > 0
    gq[...] = jnp.transpose(in_order(odd, dq[0], got[2]))
    for n, ref in ((0, gk), (1, gv)):
        total = mid[n] + rest[n] + a[n].astype(F32) + b[n].astype(F32)
        ref[...] = jnp.transpose(in_order(odd, total.astype(BF16), got[n]))


def finish(scal, dq, mid, rest, a, b, got):
    out = (TOK, 2 * ROWS)
    return pl.pallas_call(
        finish_kernel,
        grid_spec=pltpu.PrefetchScalarGridSpec(
            num_scalar_prefetch=1,
            grid=(1,),
            in_specs=[whole((1, ROWS, TOK))]
            + [whole((2, ROWS, TOK))] * 4
            + [whole((3, ROWS, TOK))],
            out_specs=[whole(out)] * 3,
        ),
        out_shape=[jax.ShapeDtypeStruct(out, BF16)] * 3,
        name="sum_and_turn",
        **params(0.1),
    )(scal, dq, mid, rest, a, b, got)


def project_kernel(norm, scal, o, o_got, dy_turned, term):
    attn = in_order(scal[2] > 0, o[0], o_got[0])
    term[...] = (mm(dy_turned[...], attn, 1, 1) * norm).astype(BF16)


def project(scal, o, o_got, dy_turned, norm):
    out = (dy_turned.shape[0], 2 * ROWS)
    return pl.pallas_call(
        functools.partial(project_kernel, norm),
        grid_spec=pltpu.PrefetchScalarGridSpec(
            num_scalar_prefetch=1,
            grid=(1,),
            in_specs=[whole((1, ROWS, TOK))] * 2 + [whole(dy_turned.shape)],
            out_specs=whole(out),
        ),
        out_shape=jax.ShapeDtypeStruct(out, BF16),
        name="projection_term",
        **params(4),
    )(scal, o, o_got, dy_turned)


def shards(queries, keys, values, grad_out, out_proj):
    me = lax.axis_index("ctx")
    blocks = lax.axis_size("ctx")
    odd = me % 2
    below = (me >= 2).astype(jnp.int32)
    above = (me < blocks - 2).astype(jnp.int32)
    scal = jnp.stack(
        [jnp.where(odd == 0, below, above), jnp.where(odd == 0, above, below), odd]
    ).astype(jnp.int32)
    swap_pairs = [(i, i ^ 1) for i in range(blocks)]
    step_a = [(i, i + (2 if i % 2 == 0 else -2)) for i in range(blocks)]
    step_b = [(i, i - (2 if i % 2 == 0 else -2)) for i in range(blocks)]
    step_a = [(i, t) for i, t in step_a if 0 <= t < blocks]
    step_b = [(i, t) for i, t in step_b if 0 <= t < blocks]

    def swap(x):
        return lax.ppermute(x, "ctx", swap_pairs)

    def to_a(x):
        return lax.ppermute(x, "ctx", step_a)

    def to_b(x):
        return lax.ppermute(x, "ctx", step_b)

    dy = grad_out[0]
    kv_mine, kv_send = split_heads(scal, "split_kv", keys[0], values[0])
    kv_got = swap(kv_send)
    a_mine, b_mine = to_a(kv_mine), to_b(kv_mine)
    q_mine, q_send = split_heads(scal, "split_q", queries[0])
    q_got = swap(q_send)
    g_mine, g_send, dy_turned = attention_grad(scal, dy, out_proj)
    kv_got, g_send = lax.optimization_barrier((kv_got, g_send))
    g_got = swap(g_send)
    a_got, b_got = to_a(kv_got), to_b(kv_got)
    kv = (a_mine, a_got, kv_mine, kv_got, b_mine, b_got)
    q = (q_mine, q_got)
    g = (g_mine, g_got)
    early_m, early_p, stats = forward((2, 3, 4, 0), scal, q, kv, None, False, 16)
    o_mine, o_send, lse = forward((1, 5), scal, q, kv, (stats, early_m, early_p), True, 8)
    o_got = swap(o_send)
    o = (o_mine, o_send)

    pair = head_major(2)
    work = (scal, q, g, o, lse, kv)
    pa, pb, dq_m, dq_p = backward(0, ((1, 0), (1, 1), (5, 1)), *work, (pair, pair))
    arrived = (to_b(pa), to_a(pb))
    whole_pair = head_major(2, F32)
    outs = (head_major(3), pair, pair, whole_pair)
    pairs = ((3, 0), (3, 1), (0, 0), (4, 0), (4, 1), (2, 1))
    for_partner, pa, pb, mid, dq_m = backward(
        1, pairs, *work, outs, (dq_m, dq_p, *arrived), 24
    )
    got = swap(for_partner)
    back_a, back_b = to_b(pa), to_a(pb)
    rest, dq = backward(2, ((2, 0),), *work, (whole_pair,), (dq_m,), 7)

    dps = lax.axis_size("dp")
    norm = float(TOK * blocks * dps) ** (-0.5)
    term = project(scal, o_mine, o_got, dy_turned, norm)
    term = lax.all_to_all(term.reshape(dps, -1, term.shape[1]), "dp", 0, 0)
    term = jnp.sum(term.astype(F32), axis=0)
    term = term.reshape(blocks, -1, term.shape[1])
    term = lax.all_to_all(term, "ctx", 0, 0)
    proj = jnp.sum(term, axis=0)

    gq, gk, gv = finish(scal, dq, mid, rest, back_a, back_b, got)
    return gq[None], gk[None], gv[None], proj


def solution(mesh):
    rows = P("dp", "ctx", None)
    return jax.shard_map(
        shards,
        mesh=mesh,
        in_specs=(rows, rows, rows, rows, P()),
        out_specs=(rows, rows, rows, P(("dp", "ctx"), None)),
        check_vma=False,
    )
```
